512 devices in a mesh: nodes: 128 (over y, z, core), feat: 4 (over x).
Axes of the slice: x: 4, y: 8, z: 8, core: 2. Of those that a mesh axis runs over, the one named last changes fastest.
Arguments:
- features: bfloat16 [65536, 128], P('nodes', 'feat'), may hold values from -6 to 6
- band_counts: bfloat16 [512, 3, 128, 128], P('nodes'), may hold values from 0 to 3, as said below
- far_counts: bfloat16 [8192, 128, 128], P('nodes'), may hold values from 0 to 3, as said below
- far_row: int32 [8192], P('nodes'), may hold values from 0 to 3
- far_src: int32 [8192], P('nodes'), may hold values from 0 to 127, as said below
- export_block: int32 [128], P('nodes'), may hold values from 0 to 3
- w_self: bfloat16 [128, 256], P('feat'), may hold values from -0.375 to 0.375
- w_neigh: bfloat16 [128, 256], P('feat'), may hold values from -0.375 to 0.375
- bias: float32 [256], P('feat'), may hold values from -3 to 3
- cotangent: bfloat16 [65536, 256], P('nodes', 'feat')
Outputs:
- hidden: bfloat16 [65536, 256], P('nodes', 'feat')
- grad_features: bfloat16 [65536, 128], P('nodes', 'feat')
- grad_self: float32 [128, 256], P('feat')
- grad_neigh: float32 [128, 256], P('feat')
- grad_bias: float32 [256], P('feat')
The draws below stay inside these ranges and needn't reach their ends.
Inputs may be any that keep to these rules, and one draw needn't show every extreme that they name: Whole numbers; the diagonal of band_counts[g, 1] is at least 1; blocks that would lie outside the slab (band_counts[0, 0] and band_counts[511, 2]) are zero. `far_counts`: whole numbers. far_src[f] differs from the index of nodes that holds block f, f // 64; the 64 blocks of one index of nodes name 64 different sources.
All inputs are finite; a program needn't handle non-finite values.
Results may differ from the reference program's by a relative error of at most 0.0044.
The reference program's roundings to bfloat16 on the way (of `aggregate`, `grad_low` and `scaled`) count: a program that leaves them out, or rounds other values in their place, can miss the bound.
Values may be sent and summed in bfloat16 or wider, within the bound.
A program may use at most 64 MiB of HBM per device.

```python
import jax
import jax.numpy as jnp
from jax import lax

FIN = 128
HID = 256
BLK = 128
ROWBLK = 4
FAR = 64
NB = 512
NODES = 65536
FARS = 8192
N_NODES = 128


def sparse_counts(key, shape, spacing):
    first, second = jax.random.split(key)
    struck = jax.random.randint(first, shape, 0, spacing) == 0
    values = jax.random.randint(second, shape, 1, 4)
    return jnp.where(struck, values, 0)


def draw_band_counts(key, part):
    key = jax.random.fold_in(key, 11)
    counts = sparse_counts(key, (NB, 3, BLK, BLK), 8)
    diagonal = jnp.arange(BLK)[:, None] == jnp.arange(BLK)[None, :]
    middle = (jnp.arange(3) == 1)[:, None, None] & diagonal[None, :, :]
    counts = jnp.where(middle[None], jnp.maximum(counts, 1), counts)
    row_ids = jnp.arange(NB)[:, None]
    which = jnp.arange(3)[None, :]
    outside = (row_ids == 0) & (which == 0) | (row_ids == NB - 1) & (which == 2)
    counts = jnp.where(outside[:, :, None, None], 0, counts)
    return counts.astype(jnp.float32).astype(jnp.bfloat16)


def draw_far_counts(key, part):
    key = jax.random.fold_in(key, 12)
    counts = sparse_counts(key, (FARS, BLK, BLK), 6)
    return counts.astype(jnp.float32).astype(jnp.bfloat16)


def draw_far_src(key, part):
    key = jax.random.fold_in(key, 13)
    keys = jax.random.split(key, N_NODES)
    offsets = jax.vmap(lambda one: jax.random.permutation(one, N_NODES - 1)[:FAR])(keys) + 1
    owners = jnp.arange(N_NODES)[:, None]
    return ((owners + offsets) % N_NODES).reshape(FARS).astype(jnp.int32)


def draw_cotangent(key, part):
    key = jax.random.fold_in(key, 14)
    rising = 3.0 ** (jnp.arange(NODES).astype(jnp.float32) / NODES)
    base = jnp.clip(jax.random.normal(key, (NODES, HID), jnp.float32), -4.0, 4.0)
    return (base * rising[:, None]).astype(jnp.bfloat16)


def touch_ends(array, rng, low, largest):
    spot = [jax.random.randint(jax.random.fold_in(rng, axis), (), 0, length) for axis, length in enumerate(array.shape)]
    widest = array.shape.index(max(array.shape))
    next_to = spot[:widest] + [(spot[widest] + 1) % array.shape[widest]] + spot[widest + 1:]
    return array.at[tuple(spot)].set(low).at[tuple(next_to)].set(largest)


def levels(own_key, dims, cuts, low, largest):
    def one(axis_at, shards_of):
        heights = jax.random.uniform(jax.random.fold_in(jax.random.fold_in(own_key, 6), axis_at), (shards_of,), jnp.float32, low / len(cuts), largest / len(cuts))
        return jnp.repeat(jnp.exp(heights), dims[axis_at] // shards_of).reshape((-1,) + (1,) * (len(dims) - axis_at - 1))

    loudness = one(*cuts[0])
    for cut in cuts[1:]:
        loudness = loudness * one(*cut)
    return loudness


def noise(stream_key, shape, scale, reach, shards=(), held_as=jnp.bfloat16):
    drawn = scale * jax.random.normal(stream_key, shape, jnp.float32)
    if shards:
        drawn = drawn * levels(stream_key, shape, shards, -0.22, 0.18)
    return jnp.clip(drawn, -reach, reach).astype(held_as)


def setup_inputs(seed: int = 0) -> dict:
    key_list = jax.random.split(jax.random.key(seed), 11)
    features = noise(key_list[0], (NODES, FIN), 1.0, 6.0, ((0, 128), (1, 4)))
    band_counts = draw_band_counts(jax.random.fold_in(key_list[10], 71), 0)
    far_counts = draw_far_counts(jax.random.fold_in(key_list[10], 71), 0)
    far_row = touch_ends(jax.random.randint(key_list[3], (FARS,), 0, ROWBLK), jax.random.fold_in(key_list[3], 1), 0, ROWBLK - 1).astype(jnp.int32)
    far_src = draw_far_src(jax.random.fold_in(key_list[10], 71), 0)
    export_block = touch_ends(jax.random.randint(key_list[5], (N_NODES,), 0, ROWBLK), jax.random.fold_in(key_list[5], 1), 0, ROWBLK - 1).astype(jnp.int32)
    w_self = noise(key_list[6], (FIN, HID), (2 * FIN) ** -0.5, 0.375, ((0, 4),))
    w_neigh = noise(key_list[7], (FIN, HID), (2 * FIN) ** -0.5, 0.375, ((0, 4),))
    bias = noise(key_list[8], (HID,), 0.5, 3.0, ((0, 4),), jnp.float32)
    cotangent = draw_cotangent(jax.random.fold_in(key_list[10], 71), 0)
    return {"features": features, "band_counts": band_counts, "far_counts": far_counts, "far_row": far_row, "far_src": far_src, "export_block": export_block, "w_self": w_self, "w_neigh": w_neigh, "bias": bias, "cotangent": cotangent}


def reference(features, band_counts, far_counts, far_row, far_src, export_block, w_self, w_neigh, bias, cotangent):
    high = lax.Precision.HIGHEST
    blocks = features.reshape(NB, BLK, FIN)
    zero_block = jnp.zeros((1, BLK, FIN), jnp.bfloat16)
    padded = jnp.concatenate([zero_block, blocks, zero_block], 0)
    export_ids = (jnp.arange(N_NODES).astype(jnp.int32) * ROWBLK + export_block).astype(jnp.int32)
    exported = blocks[export_ids]
    block_ids = jnp.arange(ROWBLK).astype(jnp.int32)

    def forward_device(device):
        start = (device * ROWBLK).astype(jnp.int32)
        band = lax.dynamic_slice_in_dim(band_counts, start, ROWBLK, 0).astype(jnp.float32)
        near = lax.dynamic_slice_in_dim(padded, start, ROWBLK + 2, 0).astype(jnp.float32)
        window = jnp.stack([near[0:ROWBLK], near[1:ROWBLK + 1], near[2:ROWBLK + 2]], 1)
        summed = jnp.einsum("bkij,bkjc->bic", band, window, precision=high)
        fstart = (device * FAR).astype(jnp.int32)
        counts = lax.dynamic_slice_in_dim(far_counts, fstart, FAR, 0).astype(jnp.float32)
        rows_of = lax.dynamic_slice_in_dim(far_row, fstart, FAR, 0)
        sources = lax.dynamic_slice_in_dim(far_src, fstart, FAR, 0)
        far_rows = exported[sources].astype(jnp.float32)
        far_terms = jnp.einsum("fij,fjc->fic", counts, far_rows, precision=high)
        place = (rows_of[None, :] == block_ids[:, None]).astype(jnp.float32)
        summed = summed + jnp.einsum("bf,fic->bic", place, far_terms, precision=high)
        degree = jnp.sum(band, axis=(1, 3)) + jnp.dot(place, jnp.sum(counts, axis=2), precision=high)
        return summed, degree

    summed, degree = lax.map(forward_device, jnp.arange(N_NODES).astype(jnp.int32))
    degree_rows = degree.reshape(NODES, 1)
    aggregate = (summed.reshape(NODES, FIN) / degree_rows).astype(jnp.bfloat16)
    pre = jnp.dot(features, w_self, preferred_element_type=jnp.float32) + jnp.dot(aggregate, w_neigh, preferred_element_type=jnp.float32) + bias
    sigma = jax.nn.sigmoid(pre)
    hidden = (pre * sigma).astype(jnp.bfloat16)
    grad_pre = cotangent.astype(jnp.float32) * sigma * (1.0 + pre * (1.0 - sigma))
    grad_low = grad_pre.astype(jnp.bfloat16)
    grad_self = jnp.dot(features.T, grad_low, preferred_element_type=jnp.float32)
    grad_neigh = jnp.dot(aggregate.T, grad_low, preferred_element_type=jnp.float32)
    grad_bias = jnp.sum(grad_pre, 0)
    self_term = jnp.dot(grad_low, w_self.T, preferred_element_type=jnp.float32)
    neigh_term = jnp.dot(grad_low, w_neigh.T, preferred_element_type=jnp.float32)
    scaled = (neigh_term / degree_rows).astype(jnp.bfloat16).reshape(NB, BLK, FIN)

    def backward_device(device):
        start = (device * ROWBLK).astype(jnp.int32)
        band = lax.dynamic_slice_in_dim(band_counts, start, ROWBLK, 0).astype(jnp.float32)
        local = lax.dynamic_slice_in_dim(scaled, start, ROWBLK, 0).astype(jnp.float32)
        back = jnp.einsum("bkij,bic->bkjc", band, local, precision=high)
        empty = jnp.zeros((1, BLK, FIN), jnp.float32)
        spread = jnp.concatenate([back[:, 0], empty, empty], 0) + jnp.concatenate([empty, back[:, 1], empty], 0) + jnp.concatenate([empty, empty, back[:, 2]], 0)
        fstart = (device * FAR).astype(jnp.int32)
        counts = lax.dynamic_slice_in_dim(far_counts, fstart, FAR, 0).astype(jnp.float32)
        rows_of = lax.dynamic_slice_in_dim(far_row, fstart, FAR, 0)
        far_back = jnp.einsum("fij,fic->fjc", counts, local[rows_of], precision=high)
        return spread, far_back

    spread_all, far_all = lax.map(backward_device, jnp.arange(N_NODES).astype(jnp.int32))
    inner = spread_all[:, 1:ROWBLK + 1]
    nothing = jnp.zeros((1, BLK, FIN), jnp.float32)
    from_prev = jnp.concatenate([nothing, spread_all[:-1, ROWBLK + 1]], 0)
    from_next = jnp.concatenate([spread_all[1:, 0], nothing], 0)
    inner = inner.at[:, 0].add(from_prev)
    inner = inner.at[:, ROWBLK - 1].add(from_next)
    targets = (far_src * ROWBLK + export_block[far_src]).astype(jnp.int32)
    far_sum = jax.ops.segment_sum(far_all.reshape(FARS, BLK, FIN), targets, NB)
    grad_features = (self_term + inner.reshape(NODES, FIN) + far_sum.reshape(NODES, FIN)).astype(jnp.bfloat16)
    return hidden, grad_features, grad_self, grad_neigh, grad_bias
```

```python
import jax
import jax.numpy as jnp
from jax import lax
from jax.experimental import pallas as pl
from jax.experimental.pallas import tpu as pltpu
from jax.sharding import PartitionSpec as P

MESH = pl.DeviceIdType.MESH
F32 = jnp.float32
BF16 = jnp.bfloat16
LANES = 128
CORES = 2


def sides(nodes):
    chips = nodes // CORES
    z = 1
    while z * z < chips:
        z *= 2
    return chips // z, z


def dot(a, b, ca, cb, precision=None):
    return lax.dot_general(a, b, (((ca,), (cb,)), ((), ())), precision=precision, preferred_element_type=F32)


def eye(n, dtype):
    rows = lax.broadcasted_iota(jnp.int32, (n, n), 0)
    cols = lax.broadcasted_iota(jnp.int32, (n, n), 1)
    return jnp.where(rows == cols, 1.0, 0.0).astype(dtype)


def each(count, body):
    def step(i, carry):
        body(i)
        return carry

    lax.fori_loop(0, count, step, 0)


def nearest(i, size):
    k = i // 2 + 1
    return k + (i % 2) * (size - 2 * k)


class Stage:
    def __init__(self, send_sems, recv_sems, base, count, to, landing):
        self.send_sems, self.recv_sems, self.base, self.count = send_sems, recv_sems, base, count
        self.to, self.landing = to, landing

    def copy(self, i, dst=None):
        src, there, device = self.to(i)
        return pltpu.make_async_remote_copy(
            src_ref=src,
            dst_ref=there if dst is None else dst,
            send_sem=self.send_sems.at[self.base + i],
            recv_sem=self.recv_sems.at[self.base + i],
            device_id=device,
            device_id_type=MESH,
        )

    def start(self, i):
        self.copy(i).start()

    def arrive(self, i):
        self.copy(i, self.landing(i)).wait_recv()

    def start_all(self):
        each(self.count, self.start)

    def arrive_all(self):
        each(self.count, self.arrive)

    def drain(self):
        each(self.count, lambda i: self.copy(i).wait_send())


def make_kernel(ys, zs, xs, far, hid):
    nodes = ys * zs * CORES
    chips = ys * zs
    blks = xs
    half = 16
    cf = 2 * half
    ch = hid // xs
    fin = cf * xs
    groups = zs * CORES
    lane_groups = hid // LANES
    tiles = 2 * (cf // 8) * lane_groups
    per = tiles // groups
    sem_plan = {}

    def plan(name, count):
        base = sum(c for _, c in sem_plan.values())
        sem_plan[name] = (base, count)

    for name, count in (
        ("a0", zs - 1), ("a1", ys - 1), ("b0", ys - 1), ("b1", zs - 1), ("c0", ys), ("c1", zs),
        ("halo", 2), ("xq", xs - 1), ("cq", xs - 1), ("ws", xs - 1), ("wn", xs - 1), ("bias", xs - 1),
        ("agg", xs - 1), ("scaled", xs - 1), ("self", xs - 1), ("hid", xs - 1), ("gx", xs - 1),
        ("ga", groups - 1), ("gy", ys - 1), ("gz", groups - 1),
        ("core0", ys), ("core1", zs), ("p0", ys - 1), ("p1", zs - 1), ("r0", zs - 1), ("r1", ys - 1), ("out", 2),
    ):
        plan(name, count)
    n_sems = sum(c for _, c in sem_plan.values())

    scratch = dict(
        XT=((blks, cf, LANES), BF16), xq=((xs, cf, LANES), BF16),
        cT=((blks, ch, LANES), BF16), cq=((xs, ch, LANES), BF16),
        wsF=((xs, cf, hid), BF16), wnF=((xs, cf, hid), BF16), biasF=((xs, ch, LANES), F32),
        wsT=((hid, fin), BF16), wnT=((hid, fin), BF16), pre0=((hid, LANES), F32),
        e0=((CORES, chips, half, LANES), BF16), e1=((CORES, chips, half, LANES), BF16),
        halo=((2, cf, LANES), BF16),
        A=((LANES, far * LANES), BF16), band=((blks, 3, LANES, LANES), BF16),
        Lm=((blks * cf + half, far * LANES), BF16),
        near=((blks, cf + half, LANES), F32), deg=((blks, 8, LANES), F32),
        agg=((blks, cf, LANES), BF16), aq=((xs, cf, LANES), BF16),
        ss=((xs, cf, LANES), BF16), sq=((blks, cf, LANES), BF16),
        st=((xs, cf, LANES), F32), stq=((blks, cf, LANES), F32),
        hs=((xs, ch, LANES), BF16), hq=((blks, ch, LANES), BF16),
        gx=((xs, tiles + 1, 8, LANES), F32), gxr=((xs, tiles + 1, 8, LANES), F32),
        ga=((groups, per + 1, 8, LANES), F32), gar=((groups, per + 1, 8, LANES), F32),
        gb=((per + 1, 8, LANES), F32), gyr=((ys, per + 1, 8, LANES), F32),
        gt=((per, 8, LANES), F32), gzr=((groups, per, 8, LANES), F32),
        BK=((far, cf, LANES), F32),
        cs0=((chips, half, LANES), F32), cs1=((chips, half, LANES), F32),
        cr0=((chips, half, LANES), F32), cr1=((chips, half, LANES), F32),
        ps0=((chips, half, LANES), BF16), ps1=((chips, half, LANES), BF16),
        pr0=((ys, zs, half, LANES), BF16), pr1=((zs, ys, half, LANES), BF16),
        q0=((zs, half, LANES), F32), q1=((ys, half, LANES), F32),
        f0=((zs, half, LANES), F32), f1=((ys, half, LANES), F32),
        ho=((2, cf, LANES), F32), hr=((2, cf, LANES), F32),
        inner=((blks, cf, LANES), F32),
    )
    names = list(scratch)

    def kernel(
        row_s, src_s, inv_s, eb_s, feat_ref, ws_ref, wn_ref, bias_ref, cot_ref, band_hbm, far_hbm,
        hid_o, gf_o, gt_o, gb_o, *rest,
    ):
        s = dict(zip(names, rest))
        send_sems, recv_sems, far_sem, band_sem = rest[len(names):]
        n = lax.axis_index("nodes")
        x = lax.axis_index("feat")
        c = n % CORES
        z = (n // CORES) % zs
        y = n // (CORES * zs)
        o = 1 - c
        g_me = z * CORES + c

        def node(yy, zz, cc):
            return (yy * zs + zz) * CORES + cc

        def stage(name, to, landing):
            base, count = sem_plan[name]
            return Stage(send_sems, recv_sems, base, count, to, landing)

        def along_z(name, src, there, here):
            def to(i):
                d = nearest(i, zs)
                peer = (z + d) % zs
                return src(peer), there(z), (node(y, peer, c), x)

            return stage(name, to, lambda i: here((z - nearest(i, zs) + zs) % zs))

        def along_y(name, src, there, here):
            def to(i):
                d = nearest(i, ys)
                peer = (y + d) % ys
                return src(peer), there(y), (node(peer, z, c), x)

            return stage(name, to, lambda i: here((y - nearest(i, ys) + ys) % ys))

        def along_x(name, src, land):
            def to(i):
                peer = (x + i + 1) % xs
                return src(peer), land(x), (n, peer)

            return stage(name, to, lambda i: land((x - i - 1 + xs) % xs))

        def along_group(name, src, land):
            def to(i):
                peer = (g_me + i + 1) % groups
                return src(peer), land(g_me), (node(y, peer // CORES, peer % CORES), x)

            return stage(name, to, lambda i: land((g_me - i - 1 + groups) % groups))

        left, right = (n + nodes - 1) % nodes, (n + 1) % nodes

        def to_sides(name, first, last, land):
            def to(i):
                return (first, last)[i], land((1, 0)[i]), ((left, right)[i], x)

            class Sides(Stage):
                def start_all(self):
                    self.start(0)
                    self.start(1)

                def arrive_all(self):
                    self.arrive(0)
                    self.arrive(1)

                def drain(self):
                    for i in range(2):
                        self.copy(i).wait_send()

            base, count = sem_plan[name]
            return Sides(send_sems, recv_sems, base, count, to, lambda i: land((1, 0)[i]))

        def to_core(name, src, there, here):
            return stage(name, lambda i: (src(i), there(i), (node(y, z, o), x)), here)

        def start_far(f):
            cols = pl.ds(pl.multiple_of(f * LANES, LANES), LANES)
            pltpu.make_async_copy(far_hbm.at[f], s["A"].at[:, cols], far_sem).start()

        each(far, start_far)
        band_copy = pltpu.make_async_copy(band_hbm, s["band"], band_sem)
        band_copy.start()

        barrier = pltpu.get_barrier_semaphore()

        def greet(device):
            pl.semaphore_signal(barrier, inc=1, device_id=device, device_id_type=MESH)

        each(ys - 1, lambda i: greet((node((y + i + 1) % ys, z, c), x)))

        def greet_group(i):
            peer = (g_me + i + 1) % groups
            greet((node(y, peer // CORES, peer % CORES), x))

        each(groups - 1, greet_group)
        each(xs - 1, lambda i: greet((n, (x + i + 1) % xs)))
        greet((left, x))
        greet((right, x))

        eye_f = eye(cf, BF16)
        eye_h = eye(ch, BF16)
        for b in range(blks):
            rows = slice(b * LANES, (b + 1) * LANES)
            s["XT"][b] = dot(eye_f, feat_ref[rows, :], 1, 1).astype(BF16)
        eb = eb_s[0]
        mine = s["XT"][eb]
        s["e0"][c, y * zs + z] = mine[:half]
        s["e1"][c, z * ys + y] = mine[half:]
        for b in range(blks):
            rows = slice(b * LANES, (b + 1) * LANES)
            s["cT"][b] = dot(eye_h, cot_ref[rows, :], 1, 1).astype(BF16)

        pl.semaphore_wait(barrier, ys - 1 + groups - 1 + xs - 1 + 2)

        e0, e1 = s["e0"], s["e1"]
        a0 = along_z("a0", lambda p: e0.at[c, y * zs + z], lambda q: e0.at[c, y * zs + q], lambda q: e0.at[c, y * zs + q])
        a1 = along_y("a1", lambda p: e1.at[c, z * ys + y], lambda q: e1.at[c, z * ys + q], lambda q: e1.at[c, z * ys + q])
        a0.start_all()
        a1.start_all()
        halo = to_sides("halo", s["XT"].at[0], s["XT"].at[blks - 1], lambda i: s["halo"].at[i])
        halo.start_all()
        xq = along_x("xq", lambda p: s["XT"].at[p], lambda q: s["xq"].at[q])
        ws = along_x("ws", lambda p: ws_ref, lambda q: s["wsF"].at[q])
        wn = along_x("wn", lambda p: wn_ref, lambda q: s["wnF"].at[q])
        bias = along_x("bias", lambda p: bias_ref, lambda q: s["biasF"].at[q])
        cq = along_x("cq", lambda p: s["cT"].at[p], lambda q: s["cq"].at[q])
        early = (xq, ws, wn, bias, cq)
        for one in early:
            one.start_all()
        s["xq"][x] = s["XT"][x]
        s["cq"][x] = s["cT"][x]
        s["wsF"][x] = ws_ref[...]
        s["wnF"][x] = wn_ref[...]
        s["biasF"][x] = bias_ref[...]

        def row0(q):
            return e0.at[c, pl.ds(q * zs, zs)]

        def row1(q):
            return e1.at[c, pl.ds(q * ys, ys)]

        b0 = along_y("b0", lambda p: row0(y), row0, row0)
        b1 = along_z("b1", lambda p: row1(z), row1, row1)

        def near_y(i):
            return (y - nearest(i - 1, ys) * jnp.minimum(i, 1) + ys) % ys

        def near_z(i):
            return (z - nearest(i - 1, zs) * jnp.minimum(i, 1) + zs) % zs

        c0 = to_core(
            "c0", lambda i: row0(near_y(i)), lambda i: row0(near_y(i)), lambda i: e0.at[o, pl.ds(near_y(i) * zs, zs)]
        )
        c1 = to_core(
            "c1", lambda i: row1(near_z(i)), lambda i: row1(near_z(i)), lambda i: e1.at[o, pl.ds(near_z(i) * ys, ys)]
        )
        a0.arrive_all()
        b0.start_all()
        c0.start(0)
        a1.arrive_all()
        b1.start_all()
        c1.start(0)

        band_copy.wait()
        halo.arrive_all()
        ones = jnp.ones((half, LANES), BF16)
        for b in range(blks):
            total = None
            for k in range(3):
                w = b + k - 1
                block = s["halo"][0] if w < 0 else s["halo"][1] if w >= blks else s["XT"][w]
                term = dot(jnp.concatenate([block, ones], 0), s["band"][b, k], 1, 1)
                total = term if total is None else total + term
            s["near"][b] = total
        for one in early:
            one.arrive_all()
        eye_w = eye(hid, BF16)
        w_self = s["wsF"][...].reshape(fin, hid)
        w_neigh = s["wnF"][...].reshape(fin, hid)
        s["wsT"][...] = dot(eye_w, w_self, 1, 1).astype(BF16)
        s["wnT"][...] = dot(eye_w, w_neigh, 1, 1).astype(BF16)
        x_full = s["xq"][...].reshape(fin, LANES)
        s["pre0"][...] = dot(s["wsT"][...], x_full, 1, 0) + s["biasF"][...].reshape(hid, LANES)
        far_all = pltpu.make_async_copy(s["A"], s["A"], far_sem)
        far_all.wait()

        def pass_on0(i):
            b0.arrive(i)
            c0.start(i + 1)

        def pass_on1(i):
            b1.arrive(i)
            c1.start(i + 1)

        each(ys - 1, pass_on0)
        each(zs - 1, pass_on1)
        c0.arrive_all()
        c1.arrive_all()

        iota = lax.broadcasted_iota(jnp.int32, (half, LANES), 0)
        zero = jnp.zeros((half, LANES), BF16)
        step = 4

        def place(f4):
            for k in range(step):
                f = f4 * step + k
                cols = pl.ds(pl.multiple_of(f * LANES, LANES), LANES)
                src = src_s[f]
                chip = src // CORES
                core = src - chip * CORES
                sy = chip // zs
                sz = chip - sy * zs
                lo = e0[core, chip]
                hi = e1[core, sz * ys + sy]
                row = row_s[f]
                for b in range(blks):
                    here = row == b
                    s["Lm"][b * cf : b * cf + half, cols] = lax.select(here, lo, zero)
                    s["Lm"][b * cf + half : (b + 1) * cf, cols] = lax.select(here, hi, zero)
                s["Lm"][blks * cf :, cols] = jnp.where(iota == row, 1.0, 0.0).astype(BF16)

        each(far // step, place)
        far_sum = dot(s["Lm"][...], s["A"][...], 1, 1)
        for b in range(blks):
            deg = s["near"][b, cf : cf + 8] + far_sum[blks * cf + b : blks * cf + b + 1]
            s["deg"][b] = deg
            summed = s["near"][b, :cf] + far_sum[b * cf : (b + 1) * cf]
            s["agg"][b] = (summed / deg[:1]).astype(BF16)
        agg = along_x("agg", lambda p: s["agg"].at[p], lambda q: s["aq"].at[q])
        agg.start_all()
        s["aq"][x] = s["agg"][x]
        deg_row = s["deg"][x][:1]
        agg.arrive_all()

        agg_full = s["aq"][...].reshape(fin, LANES)
        pre = s["pre0"][...] + dot(s["wnT"][...], agg_full, 1, 0)
        sigma = jax.nn.sigmoid(pre)
        cot = s["cq"][...].reshape(hid, LANES).astype(F32)
        grad_pre = cot * sigma * (1.0 + pre * (1.0 - sigma))
        grad_low = grad_pre.astype(BF16)
        neigh = dot(s["wnF"][...].reshape(fin, hid), grad_low, 1, 0)
        s["ss"][...] = (neigh / deg_row).astype(BF16).reshape(xs, cf, LANES)
        scaled = along_x("scaled", lambda p: s["ss"].at[p], lambda q: s["sq"].at[q])
        scaled.start_all()
        s["sq"][x] = s["ss"][x]

        pieces = (dot(x_full, grad_low, 1, 1), dot(agg_full, grad_low, 1, 1))
        bias_row = dot(jnp.ones((8, LANES), F32), grad_pre, 1, 1, lax.Precision.HIGHEST)
        rows8 = lax.broadcasted_iota(jnp.int32, (8, LANES), 0)
        bias_tile = jnp.zeros((8, LANES), F32)
        for l in range(lane_groups):
            bias_tile = jnp.where(rows8 == l, bias_row[:, l * LANES : (l + 1) * LANES], bias_tile)
        for q in range(xs):
            t = 0
            for piece in pieces:
                for r in range(cf // 8):
                    for l in range(lane_groups):
                        at = q * cf + r * 8
                        s["gx"][q, t] = piece[at : at + 8, l * LANES : (l + 1) * LANES]
                        t += 1
            s["gx"][q, tiles] = bias_tile
        gx = along_x("gx", lambda p: s["gx"].at[p], lambda q: s["gxr"].at[q])
        gx.start_all()
        s["gxr"][x] = s["gx"][x]
        s["st"][...] = dot(s["wsF"][...].reshape(fin, hid), grad_low, 1, 0).reshape(xs, cf, LANES)
        s["hs"][...] = (pre * sigma).astype(BF16).reshape(xs, ch, LANES)
        own_term = along_x("self", lambda p: s["st"].at[p], lambda q: s["stq"].at[q])
        hidden = along_x("hid", lambda p: s["hs"].at[p], lambda q: s["hq"].at[q])
        own_term.start_all()
        hidden.start_all()
        s["stq"][x] = s["st"][x]
        s["hq"][x] = s["hs"][x]

        scaled.arrive_all()

        def back(f4):
            for k in range(step):
                f = f4 * step + k
                cols = pl.ds(pl.multiple_of(f * LANES, LANES), LANES)
                s["BK"][f] = dot(s["sq"][row_s[f]], s["A"][:, cols], 1, 0)

        each(far // step, back)

        def slot(owner):
            f = inv_s[owner]
            return jnp.maximum(f, 0), (f >= 0).astype(F32)

        def share0(i):
            def one(k):
                at = i * zs + k
                f, there = slot(at * CORES + o)
                s["cs0"][at] = s["BK"][f, :half] * there

            for k in range(zs):
                one(k)
            core0.start(i)

        def share1(i):
            for k in range(ys):
                f, there = slot((k * zs + i) * CORES + o)
                s["cs1"][i * ys + k] = s["BK"][f, half:] * there
            core1.start(i)

        def of0(ref):
            return lambda i: ref.at[pl.ds(i * zs, zs)]

        def of1(ref):
            return lambda i: ref.at[pl.ds(i * ys, ys)]

        core0 = to_core("core0", of0(s["cs0"]), of0(s["cr0"]), of0(s["cr0"]))
        core1 = to_core("core1", of1(s["cs1"]), of1(s["cr1"]), of1(s["cr1"]))
        each(ys, share0)
        each(zs, share1)

        gx.arrive_all()
        for t in range(tiles + 1):
            total = s["gxr"][0, t]
            for q in range(1, xs):
                total = total + s["gxr"][q, t]
            if t < tiles:
                s["ga"][t // per, t % per] = total
            else:
                for g in range(groups):
                    s["ga"][g, per] = total
        ga = along_group("ga", lambda p: s["ga"].at[p], lambda q: s["gar"].at[q])
        ga.start_all()
        s["gar"][g_me] = s["ga"][g_me]

        spread = [None] * (blks + 2)
        for b in range(blks):
            for k in range(3):
                term = dot(s["sq"][b], s["band"][b, k], 1, 0)
                spread[b + k] = term if spread[b + k] is None else spread[b + k] + term
        s["ho"][0] = spread[0]
        s["ho"][1] = spread[blks + 1]
        for b in range(blks):
            s["inner"][b] = spread[b + 1]
        outward = to_sides("out", s["ho"].at[0], s["ho"].at[1], lambda i: s["hr"].at[i])
        outward.start_all()

        p0 = along_y("p0", lambda p: s["ps0"].at[pl.ds(p * zs, zs)], lambda q: s["pr0"].at[q], lambda q: s["pr0"].at[q])
        p1 = along_z("p1", lambda p: s["ps1"].at[pl.ds(p * ys, ys)], lambda q: s["pr1"].at[q], lambda q: s["pr1"].at[q])

        def add0(i):
            core0.arrive(i)
            for k in range(zs):
                at = i * zs + k
                f, there = slot(at * CORES + c)
                s["ps0"][at] = (s["BK"][f, :half] * there + s["cr0"][at]).astype(BF16)

        def add1(i):
            core1.arrive(i)
            for k in range(ys):
                at = i * ys + k
                f, there = slot((k * zs + i) * CORES + c)
                s["ps1"][at] = (s["BK"][f, half:] * there + s["cr1"][at]).astype(BF16)

        each(ys, add0)
        p0.start_all()
        each(zs, add1)
        p1.start_all()
        s["pr0"][y] = s["ps0"][pl.ds(y * zs, zs)]
        s["pr1"][z] = s["ps1"][pl.ds(z * ys, ys)]

        ga.arrive_all()
        total = s["gar"][0]
        for g in range(1, groups):
            total = total + s["gar"][g]
        s["gb"][...] = total
        gy = along_y("gy", lambda p: s["gb"], lambda q: s["gyr"].at[q], lambda q: s["gyr"].at[q])
        gy.start_all()
        s["gyr"][y] = total
        gy.arrive_all()
        total = s["gyr"][0]
        for q in range(1, ys):
            total = total + s["gyr"][q]
        s["gt"][...] = total[:per]
        gb_o[...] = total[per]
        gz = along_group("gz", lambda p: s["gt"], lambda q: s["gzr"].at[q])
        gz.start_all()
        s["gzr"][g_me] = total[:per]

        def add_up(ref, count):
            total = ref[0].astype(F32)
            for q in range(1, count):
                total = total + ref[q].astype(F32)
            return total

        p0.arrive_all()
        s["q0"][...] = add_up(s["pr0"], ys)
        r0 = along_z("r0", lambda p: s["q0"].at[p], lambda q: s["f0"].at[q], lambda q: s["f0"].at[q])
        r0.start_all()
        p1.arrive_all()
        s["q1"][...] = add_up(s["pr1"], zs)
        r1 = along_y("r1", lambda p: s["q1"].at[p], lambda q: s["f1"].at[q], lambda q: s["f1"].at[q])
        r1.start_all()
        s["f0"][z] = s["q0"][z]
        s["f1"][y] = s["q1"][y]

        own_term.arrive_all()
        hidden.arrive_all()
        hid_o[...] = s["hq"][...]
        outward.arrive_all()
        gz.arrive_all()
        gt_o[...] = s["gzr"][...].reshape(tiles, 8, LANES)
        r0.arrive_all()
        r1.arrive_all()
        far_total = jnp.concatenate([add_up(s["f0"], zs), add_up(s["f1"], ys)], 0)
        for b in range(blks):
            value = s["inner"][b]
            if b == 0:
                value = value + s["hr"][0]
            if b == blks - 1:
                value = value + s["hr"][1]
            value = s["stq"][b] + value
            value = value + lax.select(eb == b, far_total, jnp.zeros_like(far_total))
            gf_o[b] = value.astype(BF16)

        for one in (
            a0, a1, halo, *early, b0, b1, c0, c1, agg, scaled, gx, own_term, hidden, core0, core1, ga, outward,
            p0, p1, gy, gz, r0, r1,
        ):
            one.drain()

    outs = (
        jax.ShapeDtypeStruct((blks, ch, LANES), BF16),
        jax.ShapeDtypeStruct((blks, cf, LANES), BF16),
        jax.ShapeDtypeStruct((tiles, 8, LANES), F32),
        jax.ShapeDtypeStruct((8, LANES), F32),
    )
    scratch_shapes = [pltpu.VMEM(shape, dtype) for shape, dtype in scratch.values()] + [
        pltpu.SemaphoreType.DMA((n_sems,)),
        pltpu.SemaphoreType.DMA((n_sems,)),
        pltpu.SemaphoreType.DMA,
        pltpu.SemaphoreType.DMA,
    ]
    smem = pl.BlockSpec(memory_space=pltpu.SMEM)
    vmem = pl.BlockSpec(memory_space=pltpu.VMEM)
    hbm = pl.BlockSpec(memory_space=pl.ANY)
    call = pl.pallas_call(
        kernel,
        out_shape=outs,
        in_specs=[smem] * 4 + [vmem] * 5 + [hbm] * 2,
        out_specs=[vmem] * 4,
        scratch_shapes=scratch_shapes,
        compiler_params=pltpu.CompilerParams(
            collective_id=0, has_side_effects=True, vmem_limit_bytes=40 * 1024 * 1024
        ),
        name="layer",
    )

    def lay_out(hid_ref, gf_ref, gt_ref, gb_ref, hid_o, gf_o, gs_o, gn_o, gb_o):
        eye_n = eye(LANES, BF16)
        for b in range(blks):
            rows = slice(b * LANES, (b + 1) * LANES)
            hid_o[rows, :] = dot(eye_n, hid_ref[b], 1, 1).astype(BF16)
            gf_o[rows, :] = dot(eye_n, gf_ref[b], 1, 1).astype(BF16)
        t = 0
        for out in (gs_o, gn_o):
            for r in range(cf // 8):
                for l in range(lane_groups):
                    out[r * 8 : (r + 1) * 8, l * LANES : (l + 1) * LANES] = gt_ref[t]
                    t += 1
        x = lax.axis_index("feat")
        row = jnp.zeros((1, ch), F32)
        for q in range(xs):
            at = q * ch
            part = gb_ref[at // LANES : at // LANES + 1, at % LANES : at % LANES + ch]
            row = jnp.where(x == q, part, row)
        gb_o[...] = row

    finish = pl.pallas_call(
        lay_out,
        out_shape=(
            jax.ShapeDtypeStruct((blks * LANES, ch), BF16),
            jax.ShapeDtypeStruct((blks * LANES, cf), BF16),
            jax.ShapeDtypeStruct((cf, hid), F32),
            jax.ShapeDtypeStruct((cf, hid), F32),
            jax.ShapeDtypeStruct((1, ch), F32),
        ),
        in_specs=[vmem] * 4,
        out_specs=[vmem] * 5,
        name="lay_out",
    )
    return call, finish


def solution(mesh):
    nodes, xs = mesh.shape["nodes"], mesh.shape["feat"]
    ys, zs = sides(nodes)

    def on_device(
        features, band_counts, far_counts, far_row, far_src, export_block, w_self, w_neigh, bias, cotangent
    ):
        far = far_counts.shape[0]
        hid = w_self.shape[1]
        call, finish = make_kernel(ys, zs, xs, far, hid)
        match = far_src[None, :] == jnp.arange(nodes, dtype=jnp.int32)[:, None]
        inverse = jnp.max(jnp.where(match, jnp.arange(far, dtype=jnp.int32)[None, :], -1), axis=1)
        wide_bias = jnp.broadcast_to(bias[:, None], (bias.shape[0], LANES))
        parts = call(
            far_row, far_src, inverse, export_block, features, w_self, w_neigh, wide_bias, cotangent,
            band_counts, far_counts,
        )
        hidden, grad_features, grad_self, grad_neigh, grad_bias = finish(*parts)
        return hidden, grad_features, grad_self, grad_neigh, grad_bias.reshape(bias.shape)

    return jax.shard_map(
        on_device,
        mesh=mesh,
        in_specs=(
            P("nodes", "feat"),
            P("nodes", None, None, None),
            P("nodes", None, None),
            P("nodes"),
            P("nodes"),
            P("nodes"),
            P("feat", None),
            P("feat", None),
            P("feat"),
            P("nodes", "feat"),
        ),
        out_specs=(
            P("nodes", "feat"),
            P("nodes", "feat"),
            P("feat", None),
            P("feat", None),
            P("feat"),
        ),
        check_vma=False,
    )
```

```python
import jax
import jax.numpy as jnp
from jax import lax
from jax.experimental import pallas as pl
from jax.experimental.pallas import tpu as pltpu
from jax.sharding import PartitionSpec as P

MESH = pl.DeviceIdType.MESH
F32 = jnp.float32
BF16 = jnp.bfloat16
LANES = 128
CORES = 2
VMEM_LIMIT = 60 * 1024 * 1024


def sides(nodes):
    chips = nodes // CORES
    z = 1
    while z * z < chips:
        z *= 2
    return chips // z, z


def dot(a, b, ca, cb, precision=None):
    return lax.dot_general(a, b, (((ca,), (cb,)), ((), ())), precision=precision, preferred_element_type=F32)


def eye(n, dtype):
    rows = lax.broadcasted_iota(jnp.int32, (n, n), 0)
    cols = lax.broadcasted_iota(jnp.int32, (n, n), 1)
    return jnp.where(rows == cols, 1.0, 0.0).astype(dtype)


def each(count, body):
    def step(i, carry):
        body(i)
        return carry

    lax.fori_loop(0, count, step, 0)


def nearest(i, size):
    k = i // 2 + 1
    return k + (i % 2) * (size - 2 * k)


class Stage:
    def __init__(self, send_sems, recv_sems, base, count, to, landing):
        self.send_sems, self.recv_sems, self.base, self.count = send_sems, recv_sems, base, count
        self.to, self.landing = to, landing

    def copy(self, i, dst=None):
        src, there, device = self.to(i)
        return pltpu.make_async_remote_copy(
            src_ref=src,
            dst_ref=there if dst is None else dst,
            send_sem=self.send_sems.at[self.base + i],
            recv_sem=self.recv_sems.at[self.base + i],
            device_id=device,
            device_id_type=MESH,
        )

    def start(self, i):
        self.copy(i).start()

    def arrive(self, i):
        self.copy(i, self.landing(i)).wait_recv()

    def start_all(self):
        each(self.count, self.start)

    def arrive_all(self):
        each(self.count, self.arrive)

    def drain(self):
        each(self.count, lambda i: self.copy(i).wait_send())


def make_kernel(ys, zs, xs, far, hid):
    nodes = ys * zs * CORES
    chips = ys * zs
    blks = xs
    half = 16
    cf = 2 * half
    ch = hid // xs
    fin = cf * xs
    groups = zs * CORES
    lane_groups = hid // LANES
    tiles = 2 * (cf // 8) * lane_groups
    per = tiles // groups
    sem_plan = {}

    def plan(name, count):
        base = sum(c for _, c in sem_plan.values())
        sem_plan[name] = (base, count)

    for name, count in (
        ("a0", zs - 1), ("a1", ys - 1), ("b0", ys - 1), ("b1", zs - 1), ("c0", ys), ("c1", zs),
        ("halo", 2), ("xq", xs - 1), ("cq", xs - 1), ("ws", xs - 1), ("wn", xs - 1), ("bias", xs - 1),
        ("agg", xs - 1), ("scaled", xs - 1), ("self", xs - 1), ("hid", xs - 1), ("gx", xs - 1),
        ("ga", groups - 1), ("gy", ys - 1), ("gz", groups - 1),
        ("core0", ys), ("core1", zs), ("p0", ys - 1), ("p1", zs - 1), ("r0", zs - 1), ("r1", ys - 1), ("out", 2),
    ):
        plan(name, count)
    n_sems = sum(c for _, c in sem_plan.values())

    scratch = dict(
        feat=((cf, blks * LANES), BF16), cot=((ch, blks * LANES), BF16), inv=((1, nodes), jnp.int32),
        XT=((blks, cf, LANES), BF16), xq=((xs, cf, LANES), BF16),
        cT=((blks, ch, LANES), BF16), cq=((xs, ch, LANES), BF16),
        wsF=((xs, cf, hid), BF16), wnF=((xs, cf, hid), BF16), biasF=((xs, 8, LANES), F32),
        wsT=((hid, fin), BF16), wnT=((hid, fin), BF16), pre0=((hid, LANES), F32),
        e0=((CORES, chips, half, LANES), BF16), e1=((CORES, chips, half, LANES), BF16),
        halo=((2, cf, LANES), BF16),
        A=((LANES, far * LANES), BF16), band=((blks, 3, LANES, LANES), BF16),
        Lm=((blks * cf + half, far * LANES), BF16),
        near=((blks, cf + half, LANES), F32), deg=((blks, 8, LANES), F32),
        agg=((blks, cf, LANES), BF16), aq=((xs, cf, LANES), BF16),
        ss=((xs, cf, LANES), BF16), sq=((blks, cf, LANES), BF16),
        st=((xs, cf, LANES), F32), stq=((blks, cf, LANES), F32),
        hs=((xs, ch, LANES), BF16), hq=((blks, ch, LANES), BF16),
        gx=((xs, tiles + 1, 8, LANES), F32), gxr=((xs, tiles + 1, 8, LANES), F32),
        ga=((groups, per + 1, 8, LANES), F32), gar=((groups, per + 1, 8, LANES), F32),
        gb=((per + 1, 8, LANES), F32), gyr=((ys, per + 1, 8, LANES), F32),
        gt=((per, 8, LANES), F32), gzr=((groups, per, 8, LANES), F32),
        BK=((far, cf, LANES), F32),
        cs0=((chips, half, LANES), F32), cs1=((chips, half, LANES), F32),
        cr0=((chips, half, LANES), F32), cr1=((chips, half, LANES), F32),
        ps0=((chips, half, LANES), BF16), ps1=((chips, half, LANES), BF16),
        pr0=((ys, zs, half, LANES), BF16), pr1=((zs, ys, half, LANES), BF16),
        q0=((zs, half, LANES), F32), q1=((ys, half, LANES), F32),
        f0=((zs, half, LANES), F32), f1=((ys, half, LANES), F32),
        ho=((2, cf, LANES), F32), hr=((2, cf, LANES), F32),
        inner=((blks, cf, LANES), F32),
    )
    names = list(scratch)

    def kernel(
        row_s, src_s, eb_s, bias_ref, src_ref, feat_hbm, cot_hbm, ws_hbm, wn_hbm, band_hbm, far_hbm,
        hid_o, gf_o, gs_o, gn_o, gb_o, *rest,
    ):
        s = dict(zip(names, rest))
        send_sems, recv_sems, local_sems, inv_s = rest[len(names):]
        n = lax.axis_index("nodes")
        x = lax.axis_index("feat")
        c = n % CORES
        z = (n // CORES) % zs
        y = n // (CORES * zs)
        o = 1 - c
        g_me = z * CORES + c

        def node(yy, zz, cc):
            return (yy * zs + zz) * CORES + cc

        def stage(name, to, landing):
            base, count = sem_plan[name]
            return Stage(send_sems, recv_sems, base, count, to, landing)

        def along_z(name, src, there, here):
            def to(i):
                d = nearest(i, zs)
                peer = (z + d) % zs
                return src(peer), there(z), (node(y, peer, c), x)

            return stage(name, to, lambda i: here((z - nearest(i, zs) + zs) % zs))

        def along_y(name, src, there, here):
            def to(i):
                d = nearest(i, ys)
                peer = (y + d) % ys
                return src(peer), there(y), (node(peer, z, c), x)

            return stage(name, to, lambda i: here((y - nearest(i, ys) + ys) % ys))

        def along_x(name, src, land):
            def to(i):
                peer = (x + i + 1) % xs
                return src(peer), land(x), (n, peer)

            return stage(name, to, lambda i: land((x - i - 1 + xs) % xs))

        def along_group(name, src, land):
            def to(i):
                peer = (g_me + i + 1) % groups
                return src(peer), land(g_me), (node(y, peer // CORES, peer % CORES), x)

            return stage(name, to, lambda i: land((g_me - i - 1 + groups) % groups))

        left, right = (n + nodes - 1) % nodes, (n + 1) % nodes

        def to_sides(name, first, last, land):
            def to(i):
                return (first, last)[i], land((1, 0)[i]), ((left, right)[i], x)

            class Sides(Stage):
                def start_all(self):
                    self.start(0)
                    self.start(1)

                def arrive_all(self):
                    self.arrive(0)
                    self.arrive(1)

                def drain(self):
                    for i in range(2):
                        self.copy(i).wait_send()

            base, count = sem_plan[name]
            return Sides(send_sems, recv_sems, base, count, to, lambda i: land((1, 0)[i]))

        def to_core(name, src, there, here):
            return stage(name, lambda i: (src(i), there(i), (node(y, z, o), x)), here)

        barrier = pltpu.get_barrier_semaphore()

        def greet(device):
            pl.semaphore_signal(barrier, inc=1, device_id=device, device_id_type=MESH)

        feat_copy = pltpu.make_async_copy(feat_hbm, s["feat"], local_sems.at[0])
        feat_copy.start()
        each(ys - 1, lambda i: greet((node((y + i + 1) % ys, z, c), x)))

        def greet_group(i):
            peer = (g_me + i + 1) % groups
            greet((node(y, peer // CORES, peer % CORES), x))

        each(groups - 1, greet_group)
        each(xs - 1, lambda i: greet((n, (x + i + 1) % xs)))
        greet((left, x))
        greet((right, x))
        cot_copy = pltpu.make_async_copy(cot_hbm, s["cot"], local_sems.at[1])
        ws_copy = pltpu.make_async_copy(ws_hbm, s["wsF"].at[x], local_sems.at[2])
        wn_copy = pltpu.make_async_copy(wn_hbm, s["wnF"].at[x], local_sems.at[3])
        band_copy = pltpu.make_async_copy(band_hbm, s["band"], local_sems.at[4])
        for one in (ws_copy, wn_copy, cot_copy, band_copy):
            one.start()

        feat_copy.wait()
        for b in range(blks):
            s["XT"][b] = s["feat"][:, b * LANES : (b + 1) * LANES]
        eb = eb_s[0]
        mine = s["XT"][eb]
        s["e0"][c, y * zs + z] = mine[:half]
        s["e1"][c, z * ys + y] = mine[half:]

        pl.semaphore_wait(barrier, ys - 1 + groups - 1 + xs - 1 + 2)

        e0, e1 = s["e0"], s["e1"]
        a0 = along_z("a0", lambda p: e0.at[c, y * zs + z], lambda q: e0.at[c, y * zs + q], lambda q: e0.at[c, y * zs + q])
        a1 = along_y("a1", lambda p: e1.at[c, z * ys + y], lambda q: e1.at[c, z * ys + q], lambda q: e1.at[c, z * ys + q])
        a0.start_all()
        a1.start_all()
        halo = to_sides("halo", s["XT"].at[0], s["XT"].at[blks - 1], lambda i: s["halo"].at[i])
        halo.start_all()
        xq = along_x("xq", lambda p: s["XT"].at[p], lambda q: s["xq"].at[q])
        ws = along_x("ws", lambda p: s["wsF"].at[x], lambda q: s["wsF"].at[q])
        wn = along_x("wn", lambda p: s["wnF"].at[x], lambda q: s["wnF"].at[q])
        bias = along_x("bias", lambda p: s["biasF"].at[x], lambda q: s["biasF"].at[q])
        cq = along_x("cq", lambda p: s["cT"].at[p], lambda q: s["cq"].at[q])
        early = (xq, ws, wn, bias, cq)
        xq.start_all()
        ws_copy.wait()
        ws.start_all()
        wn_copy.wait()
        wn.start_all()
        cot_copy.wait()
        for b in range(blks):
            s["cT"][b] = s["cot"][:, b * LANES : (b + 1) * LANES]
        cq.start_all()
        s["biasF"][x] = jnp.zeros((8, LANES), F32)
        s["biasF"][x, 0:1, 0:ch] = bias_ref[...]
        bias.start_all()
        s["xq"][x] = s["XT"][x]
        s["cq"][x] = s["cT"][x]

        def start_far(f):
            cols = pl.ds(pl.multiple_of(f * LANES, LANES), LANES)
            pltpu.make_async_copy(far_hbm.at[f], s["A"].at[:, cols], local_sems.at[5]).start()

        each(far, start_far)

        diagonal = lax.broadcasted_iota(jnp.int32, (far, far), 0) == lax.broadcasted_iota(jnp.int32, (far, far), 1)
        src_col = jnp.max(jnp.where(diagonal, src_ref[...], 0), axis=1, keepdims=True)
        owners = lax.broadcasted_iota(jnp.int32, (far, nodes), 1)
        index = lax.broadcasted_iota(jnp.int32, (far, nodes), 0)
        s["inv"][...] = jnp.max(jnp.where(src_col == owners, index, -1), axis=0, keepdims=True)
        inv_copy = pltpu.make_async_copy(s["inv"], inv_s, local_sems.at[6])
        inv_copy.start()

        def row0(q):
            return e0.at[c, pl.ds(q * zs, zs)]

        def row1(q):
            return e1.at[c, pl.ds(q * ys, ys)]

        b0 = along_y("b0", lambda p: row0(y), row0, row0)
        b1 = along_z("b1", lambda p: row1(z), row1, row1)

        def near_y(i):
            return (y - nearest(i - 1, ys) * jnp.minimum(i, 1) + ys) % ys

        def near_z(i):
            return (z - nearest(i - 1, zs) * jnp.minimum(i, 1) + zs) % zs

        c0 = to_core(
            "c0", lambda i: row0(near_y(i)), lambda i: row0(near_y(i)), lambda i: e0.at[o, pl.ds(near_y(i) * zs, zs)]
        )
        c1 = to_core(
            "c1", lambda i: row1(near_z(i)), lambda i: row1(near_z(i)), lambda i: e1.at[o, pl.ds(near_z(i) * ys, ys)]
        )
        a0.arrive_all()
        b0.start_all()
        c0.start(0)
        a1.arrive_all()
        b1.start_all()
        c1.start(0)

        band_copy.wait()
        halo.arrive_all()
        ones = jnp.ones((half, LANES), BF16)
        for b in range(blks):
            total = None
            for k in range(3):
                w = b + k - 1
                block = s["halo"][0] if w < 0 else s["halo"][1] if w >= blks else s["XT"][w]
                term = dot(jnp.concatenate([block, ones], 0), s["band"][b, k], 1, 1)
                total = term if total is None else total + term
            s["near"][b] = total
        for one in early:
            one.arrive_all()
        eye_w = eye(hid, BF16)
        w_self = s["wsF"][...].reshape(fin, hid)
        w_neigh = s["wnF"][...].reshape(fin, hid)
        s["wsT"][...] = dot(eye_w, w_self, 1, 1).astype(BF16)
        s["wnT"][...] = dot(eye_w, w_neigh, 1, 1).astype(BF16)
        x_full = s["xq"][...].reshape(fin, LANES)
        own_part = dot(s["wsT"][...], x_full, 1, 0)
        eye_h = eye(ch, F32)
        for q in range(xs):
            bias_col = jnp.sum(s["biasF"][q, 0:1, 0:ch] * eye_h, axis=1, keepdims=True)
            s["pre0"][q * ch : (q + 1) * ch] = own_part[q * ch : (q + 1) * ch] + bias_col
        far_all = pltpu.make_async_copy(s["A"], s["A"], local_sems.at[5])
        far_all.wait()
        inv_copy.wait()

        def pass_on0(i):
            b0.arrive(i)
            c0.start(i + 1)

        def pass_on1(i):
            b1.arrive(i)
            c1.start(i + 1)

        each(ys - 1, pass_on0)
        each(zs - 1, pass_on1)
        c0.arrive_all()
        c1.arrive_all()

        iota = lax.broadcasted_iota(jnp.int32, (half, LANES), 0)
        zero = jnp.zeros((half, LANES), BF16)
        step = 4

        def place(f4):
            for k in range(step):
                f = f4 * step + k
                cols = pl.ds(pl.multiple_of(f * LANES, LANES), LANES)
                src = src_s[f]
                chip = src // CORES
                core = src - chip * CORES
                sy = chip // zs
                sz = chip - sy * zs
                lo = e0[core, chip]
                hi = e1[core, sz * ys + sy]
                row = row_s[f]
                for b in range(blks):
                    here = row == b
                    s["Lm"][b * cf : b * cf + half, cols] = lax.select(here, lo, zero)
                    s["Lm"][b * cf + half : (b + 1) * cf, cols] = lax.select(here, hi, zero)
                s["Lm"][blks * cf :, cols] = jnp.where(iota == row, 1.0, 0.0).astype(BF16)

        each(far // step, place)
        far_sum = dot(s["Lm"][...], s["A"][...], 1, 1)
        for b in range(blks):
            deg = s["near"][b, cf : cf + 8] + far_sum[blks * cf + b : blks * cf + b + 1]
            s["deg"][b] = deg
            summed = s["near"][b, :cf] + far_sum[b * cf : (b + 1) * cf]
            s["agg"][b] = (summed / deg[:1]).astype(BF16)
        agg = along_x("agg", lambda p: s["agg"].at[p], lambda q: s["aq"].at[q])
        agg.start_all()
        s["aq"][x] = s["agg"][x]
        deg_row = s["deg"][x][:1]
        agg.arrive_all()

        agg_full = s["aq"][...].reshape(fin, LANES)
        pre = s["pre0"][...] + dot(s["wnT"][...], agg_full, 1, 0)
        sigma = jax.nn.sigmoid(pre)
        cot = s["cq"][...].reshape(hid, LANES).astype(F32)
        grad_pre = cot * sigma * (1.0 + pre * (1.0 - sigma))
        grad_low = grad_pre.astype(BF16)
        neigh = dot(s["wnF"][...].reshape(fin, hid), grad_low, 1, 0)
        s["ss"][...] = (neigh / deg_row).astype(BF16).reshape(xs, cf, LANES)
        scaled = along_x("scaled", lambda p: s["ss"].at[p], lambda q: s["sq"].at[q])
        scaled.start_all()
        s["sq"][x] = s["ss"][x]

        pieces = (dot(x_full, grad_low, 1, 1), dot(agg_full, grad_low, 1, 1))
        bias_row = dot(jnp.ones((8, LANES), F32), grad_pre, 1, 1, lax.Precision.HIGHEST)
        rows8 = lax.broadcasted_iota(jnp.int32, (8, LANES), 0)
        bias_tile = jnp.zeros((8, LANES), F32)
        for l in range(lane_groups):
            bias_tile = jnp.where(rows8 == l, bias_row[:, l * LANES : (l + 1) * LANES], bias_tile)
        for q in range(xs):
            t = 0
            for piece in pieces:
                for r in range(cf // 8):
                    for l in range(lane_groups):
                        at = q * cf + r * 8
                        s["gx"][q, t] = piece[at : at + 8, l * LANES : (l + 1) * LANES]
                        t += 1
            s["gx"][q, tiles] = bias_tile
        gx = along_x("gx", lambda p: s["gx"].at[p], lambda q: s["gxr"].at[q])
        gx.start_all()
        s["gxr"][x] = s["gx"][x]
        s["st"][...] = dot(s["wsF"][...].reshape(fin, hid), grad_low, 1, 0).reshape(xs, cf, LANES)
        s["hs"][...] = (pre * sigma).astype(BF16).reshape(xs, ch, LANES)
        own_term = along_x("self", lambda p: s["st"].at[p], lambda q: s["stq"].at[q])
        hidden = along_x("hid", lambda p: s["hs"].at[p], lambda q: s["hq"].at[q])
        own_term.start_all()
        hidden.start_all()
        s["stq"][x] = s["st"][x]
        s["hq"][x] = s["hs"][x]

        scaled.arrive_all()

        def back(f4):
            for k in range(step):
                f = f4 * step + k
                cols = pl.ds(pl.multiple_of(f * LANES, LANES), LANES)
                s["BK"][f] = dot(s["sq"][row_s[f]], s["A"][:, cols], 1, 0)

        each(far // step, back)

        def slot(owner):
            f = inv_s[0, owner]
            return jnp.minimum(jnp.maximum(f, 0), far - 1), (f >= 0).astype(F32)

        def share0(i):
            def one(k):
                at = i * zs + k
                f, there = slot(at * CORES + o)
                s["cs0"][at] = s["BK"][f, :half] * there

            for k in range(zs):
                one(k)
            core0.start(i)

        def share1(i):
            for k in range(ys):
                f, there = slot((k * zs + i) * CORES + o)
                s["cs1"][i * ys + k] = s["BK"][f, half:] * there
            core1.start(i)

        def of0(ref):
            return lambda i: ref.at[pl.ds(i * zs, zs)]

        def of1(ref):
            return lambda i: ref.at[pl.ds(i * ys, ys)]

        core0 = to_core("core0", of0(s["cs0"]), of0(s["cr0"]), of0(s["cr0"]))
        core1 = to_core("core1", of1(s["cs1"]), of1(s["cr1"]), of1(s["cr1"]))
        each(ys, share0)
        each(zs, share1)

        gx.arrive_all()
        for t in range(tiles + 1):
            total = s["gxr"][0, t]
            for q in range(1, xs):
                total = total + s["gxr"][q, t]
            if t < tiles:
                s["ga"][t // per, t % per] = total
            else:
                for g in range(groups):
                    s["ga"][g, per] = total
        ga = along_group("ga", lambda p: s["ga"].at[p], lambda q: s["gar"].at[q])
        ga.start_all()
        s["gar"][g_me] = s["ga"][g_me]

        spread = [None] * (blks + 2)
        for b in range(blks):
            for k in range(3):
                term = dot(s["sq"][b], s["band"][b, k], 1, 0)
                spread[b + k] = term if spread[b + k] is None else spread[b + k] + term
        s["ho"][0] = spread[0]
        s["ho"][1] = spread[blks + 1]
        for b in range(blks):
            s["inner"][b] = spread[b + 1]
        outward = to_sides("out", s["ho"].at[0], s["ho"].at[1], lambda i: s["hr"].at[i])
        outward.start_all()

        p0 = along_y("p0", lambda p: s["ps0"].at[pl.ds(p * zs, zs)], lambda q: s["pr0"].at[q], lambda q: s["pr0"].at[q])
        p1 = along_z("p1", lambda p: s["ps1"].at[pl.ds(p * ys, ys)], lambda q: s["pr1"].at[q], lambda q: s["pr1"].at[q])

        def add0(i):
            core0.arrive(i)
            for k in range(zs):
                at = i * zs + k
                f, there = slot(at * CORES + c)
                s["ps0"][at] = (s["BK"][f, :half] * there + s["cr0"][at]).astype(BF16)

        def add1(i):
            core1.arrive(i)
            for k in range(ys):
                at = i * ys + k
                f, there = slot((k * zs + i) * CORES + c)
                s["ps1"][at] = (s["BK"][f, half:] * there + s["cr1"][at]).astype(BF16)

        each(ys, add0)
        p0.start_all()
        each(zs, add1)
        p1.start_all()
        s["pr0"][y] = s["ps0"][pl.ds(y * zs, zs)]
        s["pr1"][z] = s["ps1"][pl.ds(z * ys, ys)]

        ga.arrive_all()
        total = s["gar"][0]
        for g in range(1, groups):
            total = total + s["gar"][g]
        s["gb"][...] = total
        gy = along_y("gy", lambda p: s["gb"], lambda q: s["gyr"].at[q], lambda q: s["gyr"].at[q])
        gy.start_all()
        s["gyr"][y] = total
        gy.arrive_all()
        total = s["gyr"][0]
        for q in range(1, ys):
            total = total + s["gyr"][q]
        s["gt"][...] = total[:per]
        gb_row = jnp.zeros((1, ch), F32)
        for q in range(xs):
            at = q * ch
            part = total[per, at // LANES : at // LANES + 1, at % LANES : at % LANES + ch]
            gb_row = jnp.where(x == q, part, gb_row)
        gb_o[...] = gb_row
        gz = along_group("gz", lambda p: s["gt"], lambda q: s["gzr"].at[q])
        gz.start_all()
        s["gzr"][g_me] = total[:per]

        def add_up(ref, count):
            total = ref[0].astype(F32)
            for q in range(1, count):
                total = total + ref[q].astype(F32)
            return total

        p0.arrive_all()
        s["q0"][...] = add_up(s["pr0"], ys)
        r0 = along_z("r0", lambda p: s["q0"].at[p], lambda q: s["f0"].at[q], lambda q: s["f0"].at[q])
        r0.start_all()
        p1.arrive_all()
        s["q1"][...] = add_up(s["pr1"], zs)
        r1 = along_y("r1", lambda p: s["q1"].at[p], lambda q: s["f1"].at[q], lambda q: s["f1"].at[q])
        r1.start_all()
        s["f0"][z] = s["q0"][z]
        s["f1"][y] = s["q1"][y]

        own_term.arrive_all()
        hidden.arrive_all()
        for b in range(blks):
            hid_o[:, b * LANES : (b + 1) * LANES] = s["hq"][b]
        outward.arrive_all()
        gz.arrive_all()
        t = 0
        for out in (gs_o, gn_o):
            for r in range(cf // 8):
                for l in range(lane_groups):
                    out[r * 8 : (r + 1) * 8, l * LANES : (l + 1) * LANES] = s["gzr"][t // per, t % per]
                    t += 1
        r0.arrive_all()
        r1.arrive_all()
        far_total = jnp.concatenate([add_up(s["f0"], zs), add_up(s["f1"], ys)], 0)
        for b in range(blks):
            value = s["inner"][b]
            if b == 0:
                value = value + s["hr"][0]
            if b == blks - 1:
                value = value + s["hr"][1]
            value = s["stq"][b] + value
            value = value + lax.select(eb == b, far_total, jnp.zeros_like(far_total))
            gf_o[:, b * LANES : (b + 1) * LANES] = value.astype(BF16)

        for one in (
            a0, a1, halo, *early, b0, b1, c0, c1, agg, scaled, gx, own_term, hidden, core0, core1, ga, outward,
            p0, p1, gy, gz, r0, r1,
        ):
            one.drain()

    outs = (
        jax.ShapeDtypeStruct((ch, blks * LANES), BF16),
        jax.ShapeDtypeStruct((cf, blks * LANES), BF16),
        jax.ShapeDtypeStruct((cf, hid), F32),
        jax.ShapeDtypeStruct((cf, hid), F32),
        jax.ShapeDtypeStruct((1, ch), F32),
    )
    scratch_shapes = [pltpu.VMEM(shape, dtype) for shape, dtype in scratch.values()] + [
        pltpu.SemaphoreType.DMA((n_sems,)),
        pltpu.SemaphoreType.DMA((n_sems,)),
        pltpu.SemaphoreType.DMA((7,)),
        pltpu.SMEM((1, nodes), jnp.int32),
    ]
    smem = pl.BlockSpec(memory_space=pltpu.SMEM)
    vmem = pl.BlockSpec(memory_space=pltpu.VMEM)
    hbm = pl.BlockSpec(memory_space=pl.ANY)
    call = pl.pallas_call(
        kernel,
        out_shape=outs,
        in_specs=[smem] * 3 + [vmem] * 2 + [hbm] * 6,
        out_specs=[vmem] * 5,
        scratch_shapes=scratch_shapes,
        compiler_params=pltpu.CompilerParams(
            collective_id=0, has_side_effects=True, vmem_limit_bytes=VMEM_LIMIT
        ),
        name="layer",
    )

    def pass_through(*refs):
        sems = refs[-1]
        copies = [pltpu.make_async_copy(refs[i], refs[i + 5], sems.at[i]) for i in range(5)]
        for one in copies:
            one.start()
        for one in copies:
            one.wait()

    finish = pl.pallas_call(
        pass_through,
        out_shape=outs,
        in_specs=[hbm] * 5,
        out_specs=[hbm] * 5,
        scratch_shapes=[pltpu.SemaphoreType.DMA((5,))],
        compiler_params=pltpu.CompilerParams(vmem_limit_bytes=VMEM_LIMIT),
        name="pass_through",
    )
    return call, finish


def solution(mesh):
    nodes, xs = mesh.shape["nodes"], mesh.shape["feat"]
    ys, zs = sides(nodes)

    def on_device(
        features, band_counts, far_counts, far_row, far_src, export_block, w_self, w_neigh, bias, cotangent
    ):
        far = far_counts.shape[0]
        hid = w_self.shape[1]
        call, finish = make_kernel(ys, zs, xs, far, hid)
        parts = call(
            far_row, far_src, export_block, bias.reshape(1, -1), far_src.reshape(1, -1), features.T, cotangent.T,
            w_self, w_neigh, band_counts, far_counts,
        )
        hidden, grad_features, grad_self, grad_neigh, grad_bias = finish(*parts)
        return hidden.T, grad_features.T, grad_self, grad_neigh, grad_bias.reshape(bias.shape)

    return jax.shard_map(
        on_device,
        mesh=mesh,
        in_specs=(
            P("nodes", "feat"),
            P("nodes", None, None, None),
            P("nodes", None, None),
            P("nodes"),
            P("nodes"),
            P("nodes"),
            P("feat", None),
            P("feat", None),
            P("feat"),
            P("nodes", "feat"),
        ),
        out_specs=(
            P("nodes", "feat"),
            P("nodes", "feat"),
            P("feat", None),
            P("feat", None),
            P("feat"),
        ),
        check_vma=False,
    )
```

```python
import jax
import jax.numpy as jnp
from jax import lax
from jax.experimental import pallas as pl
from jax.experimental.pallas import tpu as pltpu
from jax.sharding import PartitionSpec as P

MESH = pl.DeviceIdType.MESH
F32 = jnp.float32
BF16 = jnp.bfloat16
LANES = 128
CORES = 2
VMEM_LIMIT = 60 * 1024 * 1024


def sides(nodes):
    chips = nodes // CORES
    z = 1
    while z * z < chips:
        z *= 2
    return chips // z, z


def dot(a, b, ca, cb, precision=None):
    return lax.dot_general(a, b, (((ca,), (cb,)), ((), ())), precision=precision, preferred_element_type=F32)


def eye(n, dtype):
    rows = lax.broadcasted_iota(jnp.int32, (n, n), 0)
    cols = lax.broadcasted_iota(jnp.int32, (n, n), 1)
    return jnp.where(rows == cols, 1.0, 0.0).astype(dtype)


def each(count, body):
    def step(i, carry):
        body(i)
        return carry

    lax.fori_loop(0, count, step, 0)


def nearest(i, size):
    k = lax.div(i, 2) + 1
    return k + lax.rem(i, 2) * (size - 2 * k)


class Stage:
    def __init__(self, send_sems, recv_sems, base, count, to, landing):
        self.send_sems, self.recv_sems, self.base, self.count = send_sems, recv_sems, base, count
        self.to, self.landing = to, landing

    def copy(self, i, dst=None):
        src, there, device = self.to(i)
        return pltpu.make_async_remote_copy(
            src_ref=src,
            dst_ref=there if dst is None else dst,
            send_sem=self.send_sems.at[self.base + i],
            recv_sem=self.recv_sems.at[self.base + i],
            device_id=device,
            device_id_type=MESH,
        )

    def start(self, i):
        self.copy(i).start()

    def arrive(self, i):
        self.copy(i, self.landing(i)).wait_recv()

    def start_all(self):
        each(self.count, self.start)

    def arrive_all(self):
        each(self.count, self.arrive)

    def drain(self):
        each(self.count, lambda i: self.copy(i).wait_send())


def make_kernel(ys, zs, xs, far, hid):
    nodes = ys * zs * CORES
    chips = ys * zs
    blks = xs
    half = 16
    cf = 2 * half
    ch = hid // xs
    fin = cf * xs
    groups = zs * CORES
    lane_groups = hid // LANES
    tiles = 2 * (cf // 8) * lane_groups
    per = tiles // groups
    sem_plan = {}

    def plan(name, count):
        base = sum(c for _, c in sem_plan.values())
        sem_plan[name] = (base, count)

    for name, count in (
        ("a0", zs - 1), ("a1", ys - 1), ("b0", ys - 1), ("b1", zs - 1), ("c0", ys), ("c1", zs),
        ("halo", 2), ("xq", xs - 1), ("cq", xs - 1), ("ws", xs - 1), ("wn", xs - 1), ("bias", xs - 1),
        ("agg", xs - 1), ("scaled", xs - 1), ("self", xs - 1), ("hid", xs - 1), ("gx", xs - 1),
        ("ga", groups - 1), ("gy", ys - 1), ("gz", groups - 1),
        ("core0", ys), ("core1", zs), ("p0", ys - 1), ("p1", zs - 1), ("r0", zs - 1), ("r1", ys - 1), ("out", 2),
    ):
        plan(name, count)
    n_sems = sum(c for _, c in sem_plan.values())

    scratch = dict(
        feat=((cf, blks * LANES), BF16), cot=((ch, blks * LANES), BF16), inv=((1, nodes), jnp.int32),
        srcs=((1, far), jnp.int32), bias_row=((1, ch), F32),
        hid_v=((ch, blks * LANES), BF16), gf_v=((cf, blks * LANES), BF16),
        gs_v=((cf, hid), F32), gn_v=((cf, hid), F32), gb_v=((1, ch), F32),
        XT=((blks, cf, LANES), BF16), xq=((xs, cf, LANES), BF16),
        cT=((blks, ch, LANES), BF16), cq=((xs, ch, LANES), BF16),
        wsF=((xs, cf, hid), BF16), wnF=((xs, cf, hid), BF16), biasF=((xs, 8, LANES), F32),
        wsT=((hid, fin), BF16), wnT=((hid, fin), BF16), pre0=((hid, LANES), F32),
        e0=((CORES, chips, half, LANES), BF16), e1=((CORES, chips, half, LANES), BF16),
        halo=((2, cf, LANES), BF16),
        A=((LANES, far * LANES), BF16), band=((blks, 3, LANES, LANES), BF16),
        Lm=((blks * cf + half, far * LANES), BF16),
        near=((blks, cf + half, LANES), F32), deg=((blks, 8, LANES), F32),
        agg=((blks, cf, LANES), BF16), aq=((xs, cf, LANES), BF16),
        ss=((xs, cf, LANES), BF16), sq=((blks, cf, LANES), BF16),
        st=((xs, cf, LANES), F32), stq=((blks, cf, LANES), F32),
        hs=((xs, ch, LANES), BF16), hq=((blks, ch, LANES), BF16),
        gx=((xs, tiles + 1, 8, LANES), F32), gxr=((xs, tiles + 1, 8, LANES), F32),
        ga=((groups, per + 1, 8, LANES), F32), gar=((groups, per + 1, 8, LANES), F32),
        gb=((per + 1, 8, LANES), F32), gyr=((ys, per + 1, 8, LANES), F32),
        gt=((per, 8, LANES), F32), gzr=((groups, per, 8, LANES), F32),
        BK=((far, cf, LANES), F32),
        cs0=((chips, half, LANES), F32), cs1=((chips, half, LANES), F32),
        cr0=((chips, half, LANES), F32), cr1=((chips, half, LANES), F32),
        ps0=((chips, half, LANES), BF16), ps1=((chips, half, LANES), BF16),
        pr0=((ys, zs, half, LANES), BF16), pr1=((zs, ys, half, LANES), BF16),
        q0=((zs, half, LANES), F32), q1=((ys, half, LANES), F32),
        f0=((zs, half, LANES), F32), f1=((ys, half, LANES), F32),
        ho=((2, cf, LANES), F32), hr=((2, cf, LANES), F32),
        inner=((blks, cf, LANES), F32),
    )
    names = list(scratch)

    def kernel(
        row_hbm, src_hbm, eb_hbm, bias_hbm, srcs_hbm, feat_hbm, cot_hbm, ws_hbm, wn_hbm, band_hbm, far_hbm,
        hid_hbm, gf_hbm, gs_hbm, gn_hbm, gb_hbm, *rest,
    ):
        s = dict(zip(names, rest))
        send_sems, recv_sems, local_sems, inv_s, row_s, src_s, eb_s = rest[len(names):]
        hid_o, gf_o, gs_o, gn_o, gb_o = (s[name] for name in ("hid_v", "gf_v", "gs_v", "gn_v", "gb_v"))
        n = lax.axis_index("nodes")
        x = lax.axis_index("feat")
        c = lax.rem(n, CORES)
        z = lax.rem(lax.div(n, CORES), zs)
        y = lax.div(n, CORES * zs)
        o = 1 - c
        g_me = z * CORES + c

        def node(yy, zz, cc):
            return (yy * zs + zz) * CORES + cc

        def stage(name, to, landing):
            base, count = sem_plan[name]
            return Stage(send_sems, recv_sems, base, count, to, landing)

        def offset(i, size, far_first):
            return nearest(size - 2 - i if far_first else i, size)

        def along_z(name, src, there, here, far_first=False):
            def to(i):
                peer = lax.rem(z + offset(i, zs, far_first), zs)
                return src(peer), there(z), (node(y, peer, c), x)

            return stage(name, to, lambda i: here(lax.rem(z - offset(i, zs, far_first) + zs, zs)))

        def along_y(name, src, there, here, far_first=False):
            def to(i):
                peer = lax.rem(y + offset(i, ys, far_first), ys)
                return src(peer), there(y), (node(peer, z, c), x)

            return stage(name, to, lambda i: here(lax.rem(y - offset(i, ys, far_first) + ys, ys)))

        def across(i, size):
            return 1 + lax.rem(i + size // 2 - 1, size - 1)

        def along_x(name, src, land):
            def to(i):
                peer = lax.rem(x + across(i, xs), xs)
                return src(peer), land(x), (n, peer)

            return stage(name, to, lambda i: land(lax.rem(x - across(i, xs) + xs, xs)))

        def along_group(name, src, land):
            def to(i):
                peer = lax.rem(g_me + across(i, groups), groups)
                return src(peer), land(g_me), (node(y, lax.div(peer, CORES), lax.rem(peer, CORES)), x)

            return stage(name, to, lambda i: land(lax.rem(g_me - across(i, groups) + groups, groups)))

        left, right = lax.rem(n + nodes - 1, nodes), lax.rem(n + 1, nodes)

        def to_sides(name, first, last, land):
            def to(i):
                return (first, last)[i], land((1, 0)[i]), ((left, right)[i], x)

            class Sides(Stage):
                def start_all(self):
                    self.start(0)
                    self.start(1)

                def arrive_all(self):
                    self.arrive(0)
                    self.arrive(1)

                def drain(self):
                    for i in range(2):
                        self.copy(i).wait_send()

            base, count = sem_plan[name]
            return Sides(send_sems, recv_sems, base, count, to, lambda i: land((1, 0)[i]))

        def to_core(name, src, there, here):
            return stage(name, lambda i: (src(i), there(i), (node(y, z, o), x)), here)

        barrier = pltpu.get_barrier_semaphore()

        def greet(device):
            pl.semaphore_signal(barrier, inc=1, device_id=device, device_id_type=MESH)

        def greet_group(i):
            peer = lax.rem(g_me + across(i, groups), groups)
            greet((node(y, lax.div(peer, CORES), lax.rem(peer, CORES)), x))

        def fetch(src, dst, sem):
            one = pltpu.make_async_copy(src, dst, local_sems.at[sem])
            one.start()
            return one

        each(ys - 1, lambda i: greet((node(lax.rem(y + offset(i, ys, True), ys), z, c), x)))
        feat_copy = fetch(feat_hbm, s["feat"], 0)
        eb_copy = fetch(eb_hbm, eb_s, 7)
        each(groups - 1, greet_group)
        each(xs - 1, lambda i: greet((n, lax.rem(x + i + 1, xs))))
        greet((left, x))
        greet((right, x))
        ws_copy = fetch(ws_hbm, s["wsF"].at[x], 2)
        wn_copy = fetch(wn_hbm, s["wnF"].at[x], 3)
        cot_copy = fetch(cot_hbm, s["cot"], 1)
        bias_copy = fetch(bias_hbm, s["bias_row"], 8)
        srcs_copy = fetch(srcs_hbm, s["srcs"], 9)
        band_copy = fetch(band_hbm, s["band"], 4)
        row_copy = fetch(row_hbm, row_s, 10)
        src_copy = fetch(src_hbm, src_s, 11)

        feat_copy.wait()
        for b in range(blks):
            s["XT"][b] = s["feat"][:, b * LANES : (b + 1) * LANES]
        eb_copy.wait()
        eb = eb_s[0]
        mine = s["XT"][eb]
        s["e0"][c, y * zs + z] = mine[:half]
        s["e1"][c, z * ys + y] = mine[half:]

        pl.semaphore_wait(barrier, ys - 1 + groups - 1 + xs - 1 + 2)

        e0, e1 = s["e0"], s["e1"]
        a0 = along_z("a0", lambda p: e0.at[c, y * zs + z], *[lambda q: e0.at[c, y * zs + q]] * 2, far_first=True)
        a1 = along_y("a1", lambda p: e1.at[c, z * ys + y], *[lambda q: e1.at[c, z * ys + q]] * 2, far_first=True)
        a0.start_all()
        a1.start_all()
        halo = to_sides("halo", s["XT"].at[0], s["XT"].at[blks - 1], lambda i: s["halo"].at[i])
        halo.start_all()
        xq = along_x("xq", lambda p: s["XT"].at[p], lambda q: s["xq"].at[q])
        ws = along_x("ws", lambda p: s["wsF"].at[x], lambda q: s["wsF"].at[q])
        wn = along_x("wn", lambda p: s["wnF"].at[x], lambda q: s["wnF"].at[q])
        bias = along_x("bias", lambda p: s["biasF"].at[x], lambda q: s["biasF"].at[q])
        cq = along_x("cq", lambda p: s["cT"].at[p], lambda q: s["cq"].at[q])
        early = (xq, ws, wn, bias, cq)
        xq.start_all()
        ws_copy.wait()
        ws.start_all()
        wn_copy.wait()
        wn.start_all()
        cot_copy.wait()
        for b in range(blks):
            s["cT"][b] = s["cot"][:, b * LANES : (b + 1) * LANES]
        cq.start_all()
        s["biasF"][x] = jnp.zeros((8, LANES), F32)
        bias_copy.wait()
        s["biasF"][x, 0:1, 0:ch] = s["bias_row"][...]
        bias.start_all()
        s["xq"][x] = s["XT"][x]
        s["cq"][x] = s["cT"][x]

        def start_far(f):
            cols = pl.ds(pl.multiple_of(f * LANES, LANES), LANES)
            pltpu.make_async_copy(far_hbm.at[f], s["A"].at[:, cols], local_sems.at[5]).start()

        each(far, start_far)

        srcs_copy.wait()
        diagonal = lax.broadcasted_iota(jnp.int32, (far, far), 0) == lax.broadcasted_iota(jnp.int32, (far, far), 1)
        src_col = jnp.max(jnp.where(diagonal, s["srcs"][...], 0), axis=1, keepdims=True)
        owners = lax.broadcasted_iota(jnp.int32, (far, nodes), 1)
        index = lax.broadcasted_iota(jnp.int32, (far, nodes), 0)
        s["inv"][...] = jnp.max(jnp.where(src_col == owners, index, -1), axis=0, keepdims=True)
        inv_copy = pltpu.make_async_copy(s["inv"], inv_s, local_sems.at[6])
        inv_copy.start()

        def row0(q):
            return e0.at[c, pl.ds(q * zs, zs)]

        def row1(q):
            return e1.at[c, pl.ds(q * ys, ys)]

        b0 = along_y("b0", lambda p: row0(y), row0, row0)
        b1 = along_z("b1", lambda p: row1(z), row1, row1)

        def near_y(i):
            i = jnp.int32(i)
            return lax.rem(y - nearest(jnp.maximum(i - 1, 0), ys) * jnp.minimum(i, 1) + ys, ys)

        def near_z(i):
            i = jnp.int32(i)
            return lax.rem(z - nearest(jnp.maximum(i - 1, 0), zs) * jnp.minimum(i, 1) + zs, zs)

        c0 = to_core(
            "c0", lambda i: row0(near_y(i)), lambda i: row0(near_y(i)), lambda i: e0.at[o, pl.ds(near_y(i) * zs, zs)]
        )
        c1 = to_core(
            "c1", lambda i: row1(near_z(i)), lambda i: row1(near_z(i)), lambda i: e1.at[o, pl.ds(near_z(i) * ys, ys)]
        )
        a0.arrive_all()
        b0.start_all()
        c0.start(0)
        a1.arrive_all()
        b1.start_all()
        c1.start(0)

        band_copy.wait()
        halo.arrive_all()
        ones = jnp.ones((half, LANES), BF16)
        for b in range(blks):
            total = None
            for k in range(3):
                w = b + k - 1
                block = s["halo"][0] if w < 0 else s["halo"][1] if w >= blks else s["XT"][w]
                term = dot(jnp.concatenate([block, ones], 0), s["band"][b, k], 1, 1)
                total = term if total is None else total + term
            s["near"][b] = total
        for one in early:
            one.arrive_all()
        eye_w = eye(hid, BF16)
        w_self = s["wsF"][...].reshape(fin, hid)
        w_neigh = s["wnF"][...].reshape(fin, hid)
        s["wsT"][...] = dot(eye_w, w_self, 1, 1).astype(BF16)
        s["wnT"][...] = dot(eye_w, w_neigh, 1, 1).astype(BF16)
        x_full = s["xq"][...].reshape(fin, LANES)
        own_part = dot(s["wsT"][...], x_full, 1, 0)
        eye_h = eye(ch, F32)
        for q in range(xs):
            bias_col = jnp.sum(s["biasF"][q, 0:1, 0:ch] * eye_h, axis=1, keepdims=True)
            s["pre0"][q * ch : (q + 1) * ch] = own_part[q * ch : (q + 1) * ch] + bias_col
        far_all = pltpu.make_async_copy(s["A"], s["A"], local_sems.at[5])
        far_all.wait()
        inv_copy.wait()
        row_copy.wait()
        src_copy.wait()

        def pass_on0(i):
            b0.arrive(i)
            c0.start(i + 1)

        def pass_on1(i):
            b1.arrive(i)
            c1.start(i + 1)

        each(ys - 1, pass_on0)
        each(zs - 1, pass_on1)
        c0.arrive_all()
        c1.arrive_all()

        iota = lax.broadcasted_iota(jnp.int32, (half, LANES), 0)
        zero = jnp.zeros((half, LANES), BF16)
        step = min(8, far)

        def place(f4):
            for k in range(step):
                f = f4 * step + k
                cols = pl.ds(pl.multiple_of(f * LANES, LANES), LANES)
                src = src_s[f]
                chip = lax.div(src, CORES)
                core = src - chip * CORES
                sy = lax.div(chip, zs)
                sz = chip - sy * zs
                lo = e0[core, chip]
                hi = e1[core, sz * ys + sy]
                row = row_s[f]
                for b in range(blks):
                    here = row == b
                    s["Lm"][b * cf : b * cf + half, cols] = lax.select(here, lo, zero)
                    s["Lm"][b * cf + half : (b + 1) * cf, cols] = lax.select(here, hi, zero)
                s["Lm"][blks * cf :, cols] = jnp.where(iota == row, 1.0, 0.0).astype(BF16)

        each(far // step, place)
        far_sum = dot(s["Lm"][...], s["A"][...], 1, 1)
        for b in range(blks):
            deg = s["near"][b, cf : cf + 8] + far_sum[blks * cf + b : blks * cf + b + 1]
            s["deg"][b] = deg
            summed = s["near"][b, :cf] + far_sum[b * cf : (b + 1) * cf]
            s["agg"][b] = (summed / deg[:1]).astype(BF16)
        agg = along_x("agg", lambda p: s["agg"].at[p], lambda q: s["aq"].at[q])
        agg.start_all()
        s["aq"][x] = s["agg"][x]
        deg_row = s["deg"][x][:1]
        agg.arrive_all()

        agg_full = s["aq"][...].reshape(fin, LANES)
        pre = s["pre0"][...] + dot(s["wnT"][...], agg_full, 1, 0)
        sigma = jax.nn.sigmoid(pre)
        cot = s["cq"][...].reshape(hid, LANES).astype(F32)
        grad_pre = cot * sigma * (1.0 + pre * (1.0 - sigma))
        grad_low = grad_pre.astype(BF16)
        neigh = dot(s["wnF"][...].reshape(fin, hid), grad_low, 1, 0)
        s["ss"][...] = (neigh / deg_row).astype(BF16).reshape(xs, cf, LANES)
        scaled = along_x("scaled", lambda p: s["ss"].at[p], lambda q: s["sq"].at[q])
        scaled.start_all()
        s["sq"][x] = s["ss"][x]

        pieces = (dot(x_full, grad_low, 1, 1), dot(agg_full, grad_low, 1, 1))
        bias_row = dot(jnp.ones((8, LANES), F32), grad_pre, 1, 1, lax.Precision.HIGHEST)
        rows8 = lax.broadcasted_iota(jnp.int32, (8, LANES), 0)
        bias_tile = jnp.zeros((8, LANES), F32)
        for l in range(lane_groups):
            bias_tile = jnp.where(rows8 == l, bias_row[:, l * LANES : (l + 1) * LANES], bias_tile)
        for q in range(xs):
            t = 0
            for piece in pieces:
                for r in range(cf // 8):
                    for l in range(lane_groups):
                        at = q * cf + r * 8
                        s["gx"][q, t] = piece[at : at + 8, l * LANES : (l + 1) * LANES]
                        t += 1
            s["gx"][q, tiles] = bias_tile
        gx = along_x("gx", lambda p: s["gx"].at[p], lambda q: s["gxr"].at[q])
        gx.start_all()
        s["gxr"][x] = s["gx"][x]
        s["st"][...] = dot(s["wsF"][...].reshape(fin, hid), grad_low, 1, 0).reshape(xs, cf, LANES)
        s["hs"][...] = (pre * sigma).astype(BF16).reshape(xs, ch, LANES)
        own_term = along_x("self", lambda p: s["st"].at[p], lambda q: s["stq"].at[q])
        hidden = along_x("hid", lambda p: s["hs"].at[p], lambda q: s["hq"].at[q])
        s["stq"][x] = s["st"][x]
        s["hq"][x] = s["hs"][x]

        scaled.arrive_all()

        wide = min(16, far)

        def back(f16):
            for k in range(wide):
                f = f16 * wide + k
                cols = pl.ds(pl.multiple_of(f * LANES, LANES), LANES)
                s["BK"][f] = dot(s["sq"][row_s[f]], s["A"][:, cols], 1, 0)

        each(far // wide, back)


        def slot(owner):
            f = inv_s[0, owner]
            return jnp.minimum(jnp.maximum(f, 0), far - 1), (f >= 0).astype(F32)

        def share0(i):
            def one(k):
                at = i * zs + k
                f, there = slot(at * CORES + o)
                s["cs0"][at] = s["BK"][f, :half] * there

            for k in range(zs):
                one(k)
            core0.start(i)

        def share1(i):
            for k in range(ys):
                f, there = slot((k * zs + i) * CORES + o)
                s["cs1"][i * ys + k] = s["BK"][f, half:] * there
            core1.start(i)

        def of0(ref):
            return lambda i: ref.at[pl.ds(i * zs, zs)]

        def of1(ref):
            return lambda i: ref.at[pl.ds(i * ys, ys)]

        core0 = to_core("core0", of0(s["cs0"]), of0(s["cr0"]), of0(s["cr0"]))
        core1 = to_core("core1", of1(s["cs1"]), of1(s["cr1"]), of1(s["cr1"]))
        each(ys, share0)
        each(zs, share1)

        gx.arrive_all()
        for t in range(tiles + 1):
            total = s["gxr"][0, t]
            for q in range(1, xs):
                total = total + s["gxr"][q, t]
            if t < tiles:
                s["ga"][t // per, t % per] = total
            else:
                for g in range(groups):
                    s["ga"][g, per] = total
        ga = along_group("ga", lambda p: s["ga"].at[p], lambda q: s["gar"].at[q])
        ga.start_all()
        s["gar"][g_me] = s["ga"][g_me]

        spread = [None] * (blks + 2)
        for b in range(blks):
            for k in range(3):
                term = dot(s["sq"][b], s["band"][b, k], 1, 0)
                spread[b + k] = term if spread[b + k] is None else spread[b + k] + term
        s["ho"][0] = spread[0]
        s["ho"][1] = spread[blks + 1]
        for b in range(blks):
            s["inner"][b] = spread[b + 1]
        outward = to_sides("out", s["ho"].at[0], s["ho"].at[1], lambda i: s["hr"].at[i])
        outward.start_all()

        p0 = along_y("p0", lambda p: s["ps0"].at[pl.ds(p * zs, zs)], lambda q: s["pr0"].at[q], lambda q: s["pr0"].at[q])
        p1 = along_z("p1", lambda p: s["ps1"].at[pl.ds(p * ys, ys)], lambda q: s["pr1"].at[q], lambda q: s["pr1"].at[q])

        def add0(i):
            core0.arrive(i)
            for k in range(zs):
                at = i * zs + k
                f, there = slot(at * CORES + c)
                s["ps0"][at] = (s["BK"][f, :half] * there + s["cr0"][at]).astype(BF16)

        def add1(i):
            core1.arrive(i)
            for k in range(ys):
                at = i * ys + k
                f, there = slot((k * zs + i) * CORES + c)
                s["ps1"][at] = (s["BK"][f, half:] * there + s["cr1"][at]).astype(BF16)

        each(ys, add0)
        p0.start_all()
        each(zs, add1)
        p1.start_all()
        s["pr0"][y] = s["ps0"][pl.ds(y * zs, zs)]
        s["pr1"][z] = s["ps1"][pl.ds(z * ys, ys)]

        own_term.start_all()
        hidden.start_all()
        ga.arrive_all()
        total = s["gar"][0]
        for g in range(1, groups):
            total = total + s["gar"][g]
        s["gb"][...] = total
        gy = along_y("gy", lambda p: s["gb"], *[lambda q: s["gyr"].at[q]] * 2, far_first=True)
        gy.start_all()
        s["gyr"][y] = total
        def add_up(ref, count):
            total = ref[0].astype(F32)
            for q in range(1, count):
                total = total + ref[q].astype(F32)
            return total

        p0.arrive_all()
        s["q0"][...] = add_up(s["pr0"], ys)
        r0 = along_z("r0", lambda p: s["q0"].at[p], *[lambda q: s["f0"].at[q]] * 2, far_first=True)
        r0.start_all()
        p1.arrive_all()
        s["q1"][...] = add_up(s["pr1"], zs)
        r1 = along_y("r1", lambda p: s["q1"].at[p], *[lambda q: s["f1"].at[q]] * 2, far_first=True)
        r1.start_all()
        s["f0"][z] = s["q0"][z]
        s["f1"][y] = s["q1"][y]

        gy.arrive_all()
        total = s["gyr"][0]
        for q in range(1, ys):
            total = total + s["gyr"][q]
        s["gt"][...] = total[:per]
        gb_row = jnp.zeros((1, ch), F32)
        for q in range(xs):
            at = q * ch
            part = total[per, at // LANES : at // LANES + 1, at % LANES : at % LANES + ch]
            gb_row = jnp.where(x == q, part, gb_row)
        gb_o[...] = gb_row
        gz = along_group("gz", lambda p: s["gt"], lambda q: s["gzr"].at[q])
        gz.start_all()
        s["gzr"][g_me] = total[:per]

        own_term.arrive_all()
        hidden.arrive_all()
        for b in range(blks):
            hid_o[:, b * LANES : (b + 1) * LANES] = s["hq"][b]
        hid_out = fetch(hid_o, hid_hbm, 12)
        outward.arrive_all()
        gz.arrive_all()
        t = 0
        for out in (gs_o, gn_o):
            for r in range(cf // 8):
                for l in range(lane_groups):
                    out[r * 8 : (r + 1) * 8, l * LANES : (l + 1) * LANES] = s["gzr"][t // per, t % per]
                    t += 1
        gs_out = fetch(gs_o, gs_hbm, 13)
        gn_out = fetch(gn_o, gn_hbm, 14)
        gb_out = fetch(gb_o, gb_hbm, 15)
        r0.arrive_all()
        r1.arrive_all()
        far_total = jnp.concatenate([add_up(s["f0"], zs), add_up(s["f1"], ys)], 0)
        for b in range(blks):
            value = s["inner"][b]
            if b == 0:
                value = value + s["hr"][0]
            if b == blks - 1:
                value = value + s["hr"][1]
            value = s["stq"][b] + value
            value = value + lax.select(eb == b, far_total, jnp.zeros_like(far_total))
            gf_o[:, b * LANES : (b + 1) * LANES] = value.astype(BF16)
        gf_out = fetch(gf_o, gf_hbm, 16)

        for one in (
            a0, a1, halo, *early, b0, b1, c0, c1, agg, scaled, gx, own_term, hidden, core0, core1, ga, outward,
            p0, p1, gy, gz, r0, r1,
        ):
            one.drain()
        for one in (hid_out, gs_out, gn_out, gb_out, gf_out):
            one.wait()

    outs = (
        jax.ShapeDtypeStruct((ch, blks * LANES), BF16),
        jax.ShapeDtypeStruct((cf, blks * LANES), BF16),
        jax.ShapeDtypeStruct((cf, hid), F32),
        jax.ShapeDtypeStruct((cf, hid), F32),
        jax.ShapeDtypeStruct((1, ch), F32),
    )
    scratch_shapes = [pltpu.VMEM(shape, dtype) for shape, dtype in scratch.values()] + [
        pltpu.SemaphoreType.DMA((n_sems,)),
        pltpu.SemaphoreType.DMA((n_sems,)),
        pltpu.SemaphoreType.DMA((17,)),
        pltpu.SMEM((1, nodes), jnp.int32),
        pltpu.SMEM((far,), jnp.int32),
        pltpu.SMEM((far,), jnp.int32),
        pltpu.SMEM((1,), jnp.int32),
    ]
    vmem = pl.BlockSpec(memory_space=pltpu.VMEM)
    hbm = pl.BlockSpec(memory_space=pl.ANY)
    call = pl.pallas_call(
        kernel,
        out_shape=outs,
        in_specs=[hbm] * 11,
        out_specs=[hbm] * 5,
        scratch_shapes=scratch_shapes,
        compiler_params=pltpu.CompilerParams(
            collective_id=0, has_side_effects=True, vmem_limit_bytes=VMEM_LIMIT
        ),
        name="layer",
    )

    def pass_through(*refs):
        for i in range(5):
            refs[i + 5][...] = refs[i][...]

    finish = pl.pallas_call(
        pass_through,
        out_shape=outs,
        in_specs=[vmem] * 5,
        out_specs=[vmem] * 5,
        compiler_params=pltpu.CompilerParams(vmem_limit_bytes=VMEM_LIMIT),
        name="pass_through",
    )
    return call, finish


def solution(mesh):
    nodes, xs = mesh.shape["nodes"], mesh.shape["feat"]
    ys, zs = sides(nodes)

    def on_device(
        features, band_counts, far_counts, far_row, far_src, export_block, w_self, w_neigh, bias, cotangent
    ):
        far = far_counts.shape[0]
        hid = w_self.shape[1]
        call, finish = make_kernel(ys, zs, xs, far, hid)
        parts = call(
            far_row, far_src, export_block, bias.reshape(1, -1), far_src.reshape(1, -1), features.T, cotangent.T,
            w_self, w_neigh, band_counts, far_counts,
        )
        hidden, grad_features, grad_self, grad_neigh, grad_bias = finish(*parts)
        return hidden.T, grad_features.T, grad_self, grad_neigh, grad_bias.reshape(bias.shape)

    return jax.shard_map(
        on_device,
        mesh=mesh,
        in_specs=(
            P("nodes", "feat"),
            P("nodes", None, None, None),
            P("nodes", None, None),
            P("nodes"),
            P("nodes"),
            P("nodes"),
            P("feat", None),
            P("feat", None),
            P("feat"),
            P("nodes", "feat"),
        ),
        out_specs=(
            P("nodes", "feat"),
            P("nodes", "feat"),
            P("feat", None),
            P("feat", None),
            P("feat"),
        ),
        check_vma=False,
    )
```

```python
import jax
import jax.numpy as jnp
from jax import lax
from jax.experimental import pallas as pl
from jax.experimental.pallas import tpu as pltpu
from jax.sharding import PartitionSpec as P

MESH = pl.DeviceIdType.MESH
F32 = jnp.float32
BF16 = jnp.bfloat16
LANES = 128
CORES = 2
VMEM_LIMIT = 60 * 1024 * 1024


def sides(nodes):
    chips = nodes // CORES
    z = 1
    while z * z < chips:
        z *= 2
    return chips // z, z


def dot(a, b, ca, cb, precision=None):
    return lax.dot_general(a, b, (((ca,), (cb,)), ((), ())), precision=precision, preferred_element_type=F32)


def eye(n, dtype):
    rows = lax.broadcasted_iota(jnp.int32, (n, n), 0)
    cols = lax.broadcasted_iota(jnp.int32, (n, n), 1)
    return jnp.where(rows == cols, 1.0, 0.0).astype(dtype)


def each(count, body):
    def step(i, carry):
        body(i)
        return carry

    lax.fori_loop(0, count, step, 0)


def nearest(i, size):
    k = lax.div(i, 2) + 1
    return k + lax.rem(i, 2) * (size - 2 * k)


class Stage:
    def __init__(self, send_sems, recv_sems, base, count, to, landing):
        self.send_sems, self.recv_sems, self.base, self.count = send_sems, recv_sems, base, count
        self.to, self.landing = to, landing

    def copy(self, i, dst=None):
        src, there, device = self.to(i)
        return pltpu.make_async_remote_copy(
            src_ref=src,
            dst_ref=there if dst is None else dst,
            send_sem=self.send_sems.at[self.base + i],
            recv_sem=self.recv_sems.at[self.base + i],
            device_id=device,
            device_id_type=MESH,
        )

    def start(self, i):
        self.copy(i).start()

    def arrive(self, i):
        self.copy(i, self.landing(i)).wait_recv()

    def start_all(self):
        each(self.count, self.start)

    def arrive_all(self):
        each(self.count, self.arrive)

    def drain(self):
        each(self.count, lambda i: self.copy(i).wait_send())


def make_kernel(ys, zs, xs, far, hid):
    nodes = ys * zs * CORES
    chips = ys * zs
    blks = xs
    half = 16
    cf = 2 * half
    ch = hid // xs
    fin = cf * xs
    groups = zs * CORES
    lane_groups = hid // LANES
    tiles = 2 * (cf // 8) * lane_groups
    tiles_half = tiles // CORES
    per = tiles_half // zs
    bias_at = tiles_half * 8
    sem_plan = {}

    def plan(name, count):
        base = sum(c for _, c in sem_plan.values())
        sem_plan[name] = (base, count)

    for name, count in (
        ("a0", zs - 1), ("a1", ys - 1), ("b0", ys - 1), ("b1", zs - 1), ("c0", ys), ("c1", zs),
        ("halo", 2), ("xq", xs - 1), ("cq", xs - 1), ("ws", xs - 1), ("wn", xs - 1), ("bias", xs - 1),
        ("agg", xs - 1), ("scaled", xs - 1), ("hid", xs - 1), ("gl", xs - 1), ("bt", xs - 1),
        ("gc", 1), ("ga", zs - 1), ("gy", ys - 1), ("gz", groups - 1),
        ("core0", ys), ("core1", zs), ("p0", ys - 1), ("p1", zs - 1), ("r0", zs - 1), ("r1", ys - 1), ("out", 2),
    ):
        plan(name, count)
    n_sems = sum(c for _, c in sem_plan.values())

    scratch = dict(
        feat=((cf, blks * LANES), BF16), cot=((ch, blks * LANES), BF16), inv=((1, nodes), jnp.int32),
        srcs=((1, far), jnp.int32), bias_row=((1, ch), F32),
        hid_v=((ch, blks * LANES), BF16), gf_v=((cf, blks * LANES), BF16),
        gs_v=((cf, hid), F32), gn_v=((cf, hid), F32), gb_v=((1, ch), F32),
        XT=((blks, cf, LANES), BF16), xq=((xs, cf, LANES), BF16),
        cT=((blks, ch, LANES), BF16), cq=((xs, ch, LANES), BF16),
        wsF=((xs, cf, hid), BF16), wnF=((xs, cf, hid), BF16), biasF=((xs, 8, LANES), F32),
        wsT=((hid, fin), BF16), wnT=((hid, fin), BF16), pre0=((hid, LANES), F32),
        e0=((CORES, chips, half, LANES), BF16), e1=((CORES, chips, half, LANES), BF16),
        halo=((2, cf, LANES), BF16),
        A=((LANES, far * LANES), BF16), band=((blks, 3, LANES, LANES), BF16),
        Lm=((blks * cf + half, far * LANES), BF16),
        near=((blks, cf + half, LANES), F32), deg=((blks, 8, LANES), F32),
        agg=((blks, cf, LANES), BF16), aq=((xs, cf, LANES), BF16),
        ss=((xs, cf, LANES), BF16), sq=((blks, cf, LANES), BF16),
        stq=((blks, cf, LANES), F32), gl=((blks, hid, LANES), BF16), bt=((xs, 8, LANES), F32),
        hs=((xs, ch, LANES), BF16), hq=((blks, ch, LANES), BF16),
        gh=((CORES, bias_at + 8, LANES), F32), ghr=((bias_at + 8, LANES), F32),
        ga=((zs, per * 8 + lane_groups, LANES), F32), gar=((zs, per * 8 + lane_groups, LANES), F32),
        gb=((per * 8 + lane_groups, LANES), F32), gyr=((ys, per * 8 + lane_groups, LANES), F32),
        gt=((per * 8, LANES), F32), gzr=((groups, per * 8, LANES), F32),
        BK=((far, cf, LANES), F32),
        cs0=((chips, half, LANES), BF16), cs1=((chips, half, LANES), BF16),
        cr0=((chips, half, LANES), BF16), cr1=((chips, half, LANES), BF16),
        ps0=((chips, half, LANES), BF16), ps1=((chips, half, LANES), BF16),
        pr0=((ys, zs, half, LANES), BF16), pr1=((zs, ys, half, LANES), BF16),
        q0=((zs, half, LANES), F32), q1=((ys, half, LANES), F32),
        f0=((zs, half, LANES), F32), f1=((ys, half, LANES), F32),
        ho=((2, cf, LANES), F32), hr=((2, cf, LANES), F32),
        inner=((blks, cf, LANES), F32),
    )
    names = list(scratch)

    def kernel(
        row_hbm, src_hbm, eb_hbm, bias_hbm, srcs_hbm, feat_hbm, cot_hbm, ws_hbm, wn_hbm, band_hbm, far_hbm,
        hid_hbm, gf_hbm, gs_hbm, gn_hbm, gb_hbm, *rest,
    ):
        s = dict(zip(names, rest))
        send_sems, recv_sems, local_sems, inv_s, row_s, src_s, eb_s = rest[len(names):]
        hid_o, gf_o, gs_o, gn_o, gb_o = (s[name] for name in ("hid_v", "gf_v", "gs_v", "gn_v", "gb_v"))
        n = lax.axis_index("nodes")
        x = lax.axis_index("feat")
        c = lax.rem(n, CORES)
        z = lax.rem(lax.div(n, CORES), zs)
        y = lax.div(n, CORES * zs)
        o = 1 - c
        g_me = z * CORES + c

        def node(yy, zz, cc):
            return (yy * zs + zz) * CORES + cc

        def stage(name, to, landing):
            base, count = sem_plan[name]
            return Stage(send_sems, recv_sems, base, count, to, landing)

        def offset(i, size, far_first):
            return nearest(size - 2 - i if far_first else i, size)

        def along_z(name, src, there, here, far_first=False):
            def to(i):
                peer = lax.rem(z + offset(i, zs, far_first), zs)
                return src(peer), there(z), (node(y, peer, c), x)

            return stage(name, to, lambda i: here(lax.rem(z - offset(i, zs, far_first) + zs, zs)))

        def along_y(name, src, there, here, far_first=False):
            def to(i):
                peer = lax.rem(y + offset(i, ys, far_first), ys)
                return src(peer), there(y), (node(peer, z, c), x)

            return stage(name, to, lambda i: here(lax.rem(y - offset(i, ys, far_first) + ys, ys)))

        def across(i, size):
            return 1 + lax.rem(i + size // 2 - 1, size - 1)

        def along_x(name, src, land):
            def to(i):
                peer = lax.rem(x + across(i, xs), xs)
                return src(peer), land(x), (n, peer)

            return stage(name, to, lambda i: land(lax.rem(x - across(i, xs) + xs, xs)))

        def along_group(name, src, land):
            def to(i):
                peer = lax.rem(g_me + across(i, groups), groups)
                return src(peer), land(g_me), (node(y, lax.div(peer, CORES), lax.rem(peer, CORES)), x)

            return stage(name, to, lambda i: land(lax.rem(g_me - across(i, groups) + groups, groups)))

        left, right = lax.rem(n + nodes - 1, nodes), lax.rem(n + 1, nodes)

        def to_sides(name, first, last, land):
            def to(i):
                return (first, last)[i], land((1, 0)[i]), ((left, right)[i], x)

            class Sides(Stage):
                def start_all(self):
                    self.start(0)
                    self.start(1)

                def arrive_all(self):
                    self.arrive(0)
                    self.arrive(1)

                def drain(self):
                    for i in range(2):
                        self.copy(i).wait_send()

            base, count = sem_plan[name]
            return Sides(send_sems, recv_sems, base, count, to, lambda i: land((1, 0)[i]))

        def to_core(name, src, there, here):
            return stage(name, lambda i: (src(i), there(i), (node(y, z, o), x)), here)

        barrier = pltpu.get_barrier_semaphore()

        def greet(device):
            pl.semaphore_signal(barrier, inc=1, device_id=device, device_id_type=MESH)

        def greet_group(i):
            peer = lax.rem(g_me + across(i, groups), groups)
            greet((node(y, lax.div(peer, CORES), lax.rem(peer, CORES)), x))

        def fetch(src, dst, sem):
            one = pltpu.make_async_copy(src, dst, local_sems.at[sem])
            one.start()
            return one

        each(ys - 1, lambda i: greet((node(lax.rem(y + offset(i, ys, True), ys), z, c), x)))
        feat_copy = fetch(feat_hbm, s["feat"], 0)
        eb_copy = fetch(eb_hbm, eb_s, 7)
        each(groups - 1, greet_group)
        each(xs - 1, lambda i: greet((n, lax.rem(x + i + 1, xs))))
        greet((left, x))
        greet((right, x))
        ws_copy = fetch(ws_hbm, s["wsF"].at[x], 2)
        wn_copy = fetch(wn_hbm, s["wnF"].at[x], 3)
        cot_copy = fetch(cot_hbm, s["cot"], 1)
        bias_copy = fetch(bias_hbm, s["bias_row"], 8)
        srcs_copy = fetch(srcs_hbm, s["srcs"], 9)
        band_copy = fetch(band_hbm, s["band"], 4)
        row_copy = fetch(row_hbm, row_s, 10)
        src_copy = fetch(src_hbm, src_s, 11)

        feat_copy.wait()
        for b in range(blks):
            s["XT"][b] = s["feat"][:, b * LANES : (b + 1) * LANES]
        eb_copy.wait()
        eb = eb_s[0]
        mine = s["XT"][eb]
        s["e0"][c, y * zs + z] = mine[:half]
        s["e1"][c, z * ys + y] = mine[half:]

        pl.semaphore_wait(barrier, ys - 1 + groups - 1 + xs - 1 + 2)

        e0, e1 = s["e0"], s["e1"]
        a0 = along_z("a0", lambda p: e0.at[c, y * zs + z], *[lambda q: e0.at[c, y * zs + q]] * 2, far_first=True)
        a1 = along_y("a1", lambda p: e1.at[c, z * ys + y], *[lambda q: e1.at[c, z * ys + q]] * 2, far_first=True)
        a0.start_all()
        a1.start_all()
        halo = to_sides("halo", s["XT"].at[0], s["XT"].at[blks - 1], lambda i: s["halo"].at[i])
        halo.start_all()
        xq = along_x("xq", lambda p: s["XT"].at[p], lambda q: s["xq"].at[q])
        ws = along_x("ws", lambda p: s["wsF"].at[x], lambda q: s["wsF"].at[q])
        wn = along_x("wn", lambda p: s["wnF"].at[x], lambda q: s["wnF"].at[q])
        bias = along_x("bias", lambda p: s["biasF"].at[x], lambda q: s["biasF"].at[q])
        cq = along_x("cq", lambda p: s["cT"].at[p], lambda q: s["cq"].at[q])
        early = (xq, ws, wn, bias, cq)
        xq.start_all()
        ws_copy.wait()
        ws.start_all()
        wn_copy.wait()
        wn.start_all()
        cot_copy.wait()
        for b in range(blks):
            s["cT"][b] = s["cot"][:, b * LANES : (b + 1) * LANES]
        cq.start_all()
        s["biasF"][x] = jnp.zeros((8, LANES), F32)
        bias_copy.wait()
        s["biasF"][x, 0:1, 0:ch] = s["bias_row"][...]
        bias.start_all()
        s["xq"][x] = s["XT"][x]
        s["cq"][x] = s["cT"][x]

        def start_far(f):
            cols = pl.ds(pl.multiple_of(f * LANES, LANES), LANES)
            pltpu.make_async_copy(far_hbm.at[f], s["A"].at[:, cols], local_sems.at[5]).start()

        each(far, start_far)

        srcs_copy.wait()
        diagonal = lax.broadcasted_iota(jnp.int32, (far, far), 0) == lax.broadcasted_iota(jnp.int32, (far, far), 1)
        src_col = jnp.max(jnp.where(diagonal, s["srcs"][...], 0), axis=1, keepdims=True)
        owners = lax.broadcasted_iota(jnp.int32, (far, nodes), 1)
        index = lax.broadcasted_iota(jnp.int32, (far, nodes), 0)
        s["inv"][...] = jnp.max(jnp.where(src_col == owners, index, -1), axis=0, keepdims=True)
        inv_copy = pltpu.make_async_copy(s["inv"], inv_s, local_sems.at[6])
        inv_copy.start()

        def row0(q):
            return e0.at[c, pl.ds(q * zs, zs)]

        def row1(q):
            return e1.at[c, pl.ds(q * ys, ys)]

        b0 = along_y("b0", lambda p: row0(y), row0, row0)
        b1 = along_z("b1", lambda p: row1(z), row1, row1)

        def near_y(i):
            i = jnp.int32(i)
            return lax.rem(y - nearest(jnp.maximum(i - 1, 0), ys) * jnp.minimum(i, 1) + ys, ys)

        def near_z(i):
            i = jnp.int32(i)
            return lax.rem(z - nearest(jnp.maximum(i - 1, 0), zs) * jnp.minimum(i, 1) + zs, zs)

        c0 = to_core(
            "c0", lambda i: row0(near_y(i)), lambda i: row0(near_y(i)), lambda i: e0.at[o, pl.ds(near_y(i) * zs, zs)]
        )
        c1 = to_core(
            "c1", lambda i: row1(near_z(i)), lambda i: row1(near_z(i)), lambda i: e1.at[o, pl.ds(near_z(i) * ys, ys)]
        )
        a0.arrive_all()
        b0.start_all()
        c0.start(0)
        a1.arrive_all()
        b1.start_all()
        c1.start(0)

        band_copy.wait()
        halo.arrive_all()
        ones = jnp.ones((half, LANES), BF16)
        for b in range(blks):
            total = None
            for k in range(3):
                w = b + k - 1
                block = s["halo"][0] if w < 0 else s["halo"][1] if w >= blks else s["XT"][w]
                term = dot(jnp.concatenate([block, ones], 0), s["band"][b, k], 1, 1)
                total = term if total is None else total + term
            s["near"][b] = total
        for one in early:
            one.arrive_all()
        eye_w = eye(hid, BF16)
        w_self = s["wsF"][...].reshape(fin, hid)
        w_neigh = s["wnF"][...].reshape(fin, hid)
        s["wsT"][...] = dot(eye_w, w_self, 1, 1).astype(BF16)
        s["wnT"][...] = dot(eye_w, w_neigh, 1, 1).astype(BF16)
        x_full = s["xq"][...].reshape(fin, LANES)
        own_part = dot(s["wsT"][...], x_full, 1, 0)
        eye_h = eye(ch, F32)
        for q in range(xs):
            bias_col = jnp.sum(s["biasF"][q, 0:1, 0:ch] * eye_h, axis=1, keepdims=True)
            s["pre0"][q * ch : (q + 1) * ch] = own_part[q * ch : (q + 1) * ch] + bias_col
        far_all = pltpu.make_async_copy(s["A"], s["A"], local_sems.at[5])
        far_all.wait()
        inv_copy.wait()
        row_copy.wait()
        src_copy.wait()

        for one in (a0, a1, halo, *early):
            one.drain()
        def pass_on0(i):
            b0.arrive(i)
            c0.start(i + 1)

        def pass_on1(i):
            b1.arrive(i)
            c1.start(i + 1)

        each(ys - 1, pass_on0)
        each(zs - 1, pass_on1)
        c0.arrive_all()
        c1.arrive_all()

        iota = lax.broadcasted_iota(jnp.int32, (half, LANES), 0)
        zero = jnp.zeros((half, LANES), BF16)
        step = min(8, far)

        def place(f4):
            for k in range(step):
                f = f4 * step + k
                cols = pl.ds(pl.multiple_of(f * LANES, LANES), LANES)
                src = src_s[f]
                chip = lax.div(src, CORES)
                core = src - chip * CORES
                sy = lax.div(chip, zs)
                sz = chip - sy * zs
                lo = e0[core, chip]
                hi = e1[core, sz * ys + sy]
                row = row_s[f]
                for b in range(blks):
                    here = row == b
                    s["Lm"][b * cf : b * cf + half, cols] = lax.select(here, lo, zero)
                    s["Lm"][b * cf + half : (b + 1) * cf, cols] = lax.select(here, hi, zero)
                s["Lm"][blks * cf :, cols] = jnp.where(iota == row, 1.0, 0.0).astype(BF16)

        each(far // step, place)
        far_sum = dot(s["Lm"][...], s["A"][...], 1, 1)
        for b in range(blks):
            deg = s["near"][b, cf : cf + 8] + far_sum[blks * cf + b : blks * cf + b + 1]
            s["deg"][b] = deg
            summed = s["near"][b, :cf] + far_sum[b * cf : (b + 1) * cf]
            s["agg"][b] = (summed / deg[:1]).astype(BF16)
        agg = along_x("agg", lambda p: s["agg"].at[p], lambda q: s["aq"].at[q])
        agg.start_all()
        s["aq"][x] = s["agg"][x]
        deg_row = s["deg"][x][:1]
        for one in (b0, b1, c0, c1):
            one.drain()
        agg.arrive_all()

        agg_full = s["aq"][...].reshape(fin, LANES)
        pre = s["pre0"][...] + dot(s["wnT"][...], agg_full, 1, 0)
        sigma = jax.nn.sigmoid(pre)
        cot = s["cq"][...].reshape(hid, LANES).astype(F32)
        grad_pre = cot * sigma * (1.0 + pre * (1.0 - sigma))
        grad_low = grad_pre.astype(BF16)
        neigh = dot(s["wnF"][...].reshape(fin, hid), grad_low, 1, 0)
        s["ss"][...] = (neigh / deg_row).astype(BF16).reshape(xs, cf, LANES)
        scaled = along_x("scaled", lambda p: s["ss"].at[p], lambda q: s["sq"].at[q])
        scaled.start_all()
        s["sq"][x] = s["ss"][x]

        s["gl"][x] = grad_low
        gl = along_x("gl", lambda p: s["gl"].at[x], lambda q: s["gl"].at[q])
        gl.start_all()
        bias_row = dot(jnp.ones((8, LANES), F32), grad_pre, 1, 1, lax.Precision.HIGHEST)
        rows8 = lax.broadcasted_iota(jnp.int32, (8, LANES), 0)
        bias_tile = jnp.zeros((8, LANES), F32)
        for l in range(lane_groups):
            bias_tile = jnp.where(rows8 == l, bias_row[:, l * LANES : (l + 1) * LANES], bias_tile)
        s["bt"][x] = bias_tile
        bt = along_x("bt", lambda p: s["bt"].at[x], lambda q: s["bt"].at[q])
        bt.start_all()
        s["hs"][...] = (pre * sigma).astype(BF16).reshape(xs, ch, LANES)
        s["hq"][x] = s["hs"][x]

        for one in (agg,):
            one.drain()
        scaled.arrive_all()

        wide = min(16, far)

        def back(f16):
            for k in range(wide):
                f = f16 * wide + k
                cols = pl.ds(pl.multiple_of(f * LANES, LANES), LANES)
                s["BK"][f] = dot(s["sq"][row_s[f]], s["A"][:, cols], 1, 0)

        each(far // wide, back)

        gl.arrive_all()
        bt.arrive_all()
        grads = None
        for b in range(blks):
            both = jnp.concatenate([s["XT"][b], s["agg"][b]], 0)
            term = dot(both, s["gl"][b], 1, 1)
            grads = term if grads is None else grads + term
        t = 0
        for w in range(2):
            for r in range(cf // 8):
                for l in range(lane_groups):
                    at = w * cf + r * 8
                    row = t % tiles_half * 8
                    s["gh"][t // tiles_half, row : row + 8] = grads[at : at + 8, l * LANES : (l + 1) * LANES]
                    t += 1
        bias_sum = s["bt"][0]
        for q in range(1, xs):
            bias_sum = bias_sum + s["bt"][q]
        for k in range(CORES):
            s["gh"][k, bias_at:] = bias_sum
        gc = to_core("gc", lambda i: s["gh"].at[o], lambda i: s["ghr"], lambda i: s["ghr"])
        gc.start(0)

        def slot(owner):
            f = inv_s[0, owner]
            return jnp.minimum(jnp.maximum(f, 0), far - 1), (f >= 0).astype(F32)

        def share0(i):
            def one(k):
                at = i * zs + k
                f, there = slot(at * CORES + o)
                s["cs0"][at] = (s["BK"][f, :half] * there).astype(BF16)

            for k in range(zs):
                one(k)
            core0.start(i)

        def share1(i):
            for k in range(ys):
                f, there = slot((k * zs + i) * CORES + o)
                s["cs1"][i * ys + k] = (s["BK"][f, half:] * there).astype(BF16)
            core1.start(i)

        def of0(ref):
            return lambda i: ref.at[pl.ds(i * zs, zs)]

        def of1(ref):
            return lambda i: ref.at[pl.ds(i * ys, ys)]

        core0 = to_core("core0", of0(s["cs0"]), of0(s["cr0"]), of0(s["cr0"]))
        core1 = to_core("core1", of1(s["cs1"]), of1(s["cr1"]), of1(s["cr1"]))
        each(zs, share1)
        each(ys, share0)

        spread = [None] * (blks + 2)
        for b in range(blks):
            for k in range(3):
                term = dot(s["sq"][b], s["band"][b, k], 1, 0)
                spread[b + k] = term if spread[b + k] is None else spread[b + k] + term
        s["ho"][0] = spread[0]
        s["ho"][1] = spread[blks + 1]
        for b in range(blks):
            s["inner"][b] = spread[b + 1]
        outward = to_sides("out", s["ho"].at[0], s["ho"].at[1], lambda i: s["hr"].at[i])
        gc.arrive(0)
        for k in range(zs):
            rows = slice(k * per * 8, (k + 1) * per * 8)
            s["ga"][k, : per * 8] = s["gh"][c, rows] + s["ghr"][rows]
            bias_rows = slice(bias_at, bias_at + lane_groups)
            s["ga"][k, per * 8 :] = s["gh"][c, bias_rows] + s["ghr"][bias_rows]
        ga = along_z("ga", lambda p: s["ga"].at[p], *[lambda q: s["gar"].at[q]] * 2, far_first=True)
        ga.start_all()
        s["gar"][z] = s["ga"][z]
        outward.start_all()
        own_self = s["wsF"][x]
        for b in range(blks):
            s["stq"][b] = dot(own_self, s["gl"][b], 1, 0)

        p0 = along_y("p0", lambda p: s["ps0"].at[pl.ds(p * zs, zs)], lambda q: s["pr0"].at[q], lambda q: s["pr0"].at[q])
        p1 = along_z("p1", lambda p: s["ps1"].at[pl.ds(p * ys, ys)], lambda q: s["pr1"].at[q], lambda q: s["pr1"].at[q])

        def add0(i):
            core0.arrive(i)
            for k in range(zs):
                at = i * zs + k
                f, there = slot(at * CORES + c)
                s["ps0"][at] = (s["BK"][f, :half] * there + s["cr0"][at].astype(F32)).astype(BF16)

        def add1(i):
            core1.arrive(i)
            for k in range(ys):
                at = i * ys + k
                f, there = slot((k * zs + i) * CORES + c)
                s["ps1"][at] = (s["BK"][f, half:] * there + s["cr1"][at].astype(F32)).astype(BF16)

        each(zs, add1)
        p1.start_all()
        each(ys, add0)
        p0.start_all()
        s["pr0"][y] = s["ps0"][pl.ds(y * zs, zs)]
        s["pr1"][z] = s["ps1"][pl.ds(z * ys, ys)]

        ga.arrive_all()
        total = s["gar"][0]
        for g in range(1, zs):
            total = total + s["gar"][g]
        s["gb"][...] = total
        gy = along_y("gy", lambda p: s["gb"], *[lambda q: s["gyr"].at[q]] * 2, far_first=True)
        gy.start_all()
        s["gyr"][y] = total
        def add_up(ref, count):
            total = ref[0].astype(F32)
            for q in range(1, count):
                total = total + ref[q].astype(F32)
            return total

        for one in (scaled, gl, bt, gc, core0, core1, outward, ga):
            one.drain()
        gy.arrive_all()
        total = s["gyr"][0]
        for q in range(1, ys):
            total = total + s["gyr"][q]
        s["gt"][...] = total[: per * 8]
        gb_row = jnp.zeros((1, ch), F32)
        for q in range(xs):
            at = q * ch
            row = per * 8 + at // LANES
            part = total[row : row + 1, at % LANES : at % LANES + ch]
            gb_row = jnp.where(x == q, part, gb_row)
        gb_o[...] = gb_row
        gz = along_group("gz", lambda p: s["gt"], lambda q: s["gzr"].at[q])
        gz.start_all()
        s["gzr"][g_me] = total[: per * 8]

        p1.arrive_all()
        s["q1"][...] = add_up(s["pr1"], zs)
        r1 = along_y("r1", lambda p: s["q1"].at[p], *[lambda q: s["f1"].at[q]] * 2, far_first=True)
        r1.start_all()
        p0.arrive_all()
        s["q0"][...] = add_up(s["pr0"], ys)
        r0 = along_z("r0", lambda p: s["q0"].at[p], *[lambda q: s["f0"].at[q]] * 2, far_first=True)
        r0.start_all()
        s["f0"][z] = s["q0"][z]
        s["f1"][y] = s["q1"][y]

        hidden = along_x("hid", lambda p: s["hs"].at[p], lambda q: s["hq"].at[q])
        hidden.start_all()
        for one in (p0, p1, gy):
            one.drain()
        outward.arrive_all()
        gz.arrive_all()
        t = 0
        for out in (gs_o, gn_o):
            for r in range(cf // 8):
                for l in range(lane_groups):
                    out[r * 8 : (r + 1) * 8, l * LANES : (l + 1) * LANES] = s["gzr"][
                        t % tiles_half // per * CORES + t // tiles_half, t % per * 8 : t % per * 8 + 8
                    ]
                    t += 1
        gs_out = fetch(gs_o, gs_hbm, 13)
        gn_out = fetch(gn_o, gn_hbm, 14)
        gb_out = fetch(gb_o, gb_hbm, 15)
        hidden.arrive_all()
        for b in range(blks):
            hid_o[:, b * LANES : (b + 1) * LANES] = s["hq"][b]
        hid_out = fetch(hid_o, hid_hbm, 12)
        r1.arrive_all()
        r0.arrive_all()
        far_total = jnp.concatenate([add_up(s["f0"], zs), add_up(s["f1"], ys)], 0)
        for b in range(blks):
            value = s["inner"][b]
            if b == 0:
                value = value + s["hr"][0]
            if b == blks - 1:
                value = value + s["hr"][1]
            value = s["stq"][b] + value
            value = value + lax.select(eb == b, far_total, jnp.zeros_like(far_total))
            gf_o[:, b * LANES : (b + 1) * LANES] = value.astype(BF16)
        gf_out = fetch(gf_o, gf_hbm, 16)

        for one in (gz, r0, r1, hidden):
            one.drain()
        for one in (hid_out, gs_out, gn_out, gb_out, gf_out):
            one.wait()

    outs = (
        jax.ShapeDtypeStruct((ch, blks * LANES), BF16),
        jax.ShapeDtypeStruct((cf, blks * LANES), BF16),
        jax.ShapeDtypeStruct((cf, hid), F32),
        jax.ShapeDtypeStruct((cf, hid), F32),
        jax.ShapeDtypeStruct((1, ch), F32),
    )
    scratch_shapes = [pltpu.VMEM(shape, dtype) for shape, dtype in scratch.values()] + [
        pltpu.SemaphoreType.DMA((n_sems,)),
        pltpu.SemaphoreType.DMA((n_sems,)),
        pltpu.SemaphoreType.DMA((17,)),
        pltpu.SMEM((1, nodes), jnp.int32),
        pltpu.SMEM((far,), jnp.int32),
        pltpu.SMEM((far,), jnp.int32),
        pltpu.SMEM((1,), jnp.int32),
    ]
    vmem = pl.BlockSpec(memory_space=pltpu.VMEM)
    hbm = pl.BlockSpec(memory_space=pl.ANY)
    call = pl.pallas_call(
        kernel,
        out_shape=outs,
        in_specs=[hbm] * 11,
        out_specs=[hbm] * 5,
        scratch_shapes=scratch_shapes,
        compiler_params=pltpu.CompilerParams(
            collective_id=0, has_side_effects=True, vmem_limit_bytes=VMEM_LIMIT
        ),
        name="layer",
    )

    def pass_through(*refs):
        for i in range(5):
            refs[i + 5][...] = refs[i][...]

    finish = pl.pallas_call(
        pass_through,
        out_shape=outs,
        in_specs=[vmem] * 5,
        out_specs=[vmem] * 5,
        compiler_params=pltpu.CompilerParams(vmem_limit_bytes=VMEM_LIMIT),
        name="pass_through",
    )
    return call, finish


def solution(mesh):
    nodes, xs = mesh.shape["nodes"], mesh.shape["feat"]
    ys, zs = sides(nodes)

    def on_device(
        features, band_counts, far_counts, far_row, far_src, export_block, w_self, w_neigh, bias, cotangent
    ):
        far = far_counts.shape[0]
        hid = w_self.shape[1]
        call, finish = make_kernel(ys, zs, xs, far, hid)
        parts = call(
            far_row, far_src, export_block, bias.reshape(1, -1), far_src.reshape(1, -1), features.T, cotangent.T,
            w_self, w_neigh, band_counts, far_counts,
        )
        hidden, grad_features, grad_self, grad_neigh, grad_bias = finish(*parts)
        return hidden.T, grad_features.T, grad_self, grad_neigh, grad_bias.reshape(bias.shape)

    return jax.shard_map(
        on_device,
        mesh=mesh,
        in_specs=(
            P("nodes", "feat"),
            P("nodes", None, None, None),
            P("nodes", None, None),
            P("nodes"),
            P("nodes"),
            P("nodes"),
            P("feat", None),
            P("feat", None),
            P("feat"),
            P("nodes", "feat"),
        ),
        out_specs=(
            P("nodes", "feat"),
            P("nodes", "feat"),
            P("feat", None),
            P("feat", None),
            P("feat"),
        ),
        check_vma=False,
    )
```

```python
import jax
import jax.numpy as jnp
from jax import lax
from jax.experimental import pallas as pl
from jax.experimental.pallas import tpu as pltpu
from jax.sharding import PartitionSpec as P

MESH = pl.DeviceIdType.MESH
F32 = jnp.float32
BF16 = jnp.bfloat16
LANES = 128
CORES = 2
VMEM_LIMIT = 60 * 1024 * 1024


def sides(nodes):
    chips = nodes // CORES
    z = 1
    while z * z < chips:
        z *= 2
    return chips // z, z


def dot(a, b, ca, cb, precision=None):
    return lax.dot_general(a, b, (((ca,), (cb,)), ((), ())), precision=precision, preferred_element_type=F32)


def eye(n, dtype):
    rows = lax.broadcasted_iota(jnp.int32, (n, n), 0)
    cols = lax.broadcasted_iota(jnp.int32, (n, n), 1)
    return jnp.where(rows == cols, 1.0, 0.0).astype(dtype)


def each(count, body):
    def step(i, carry):
        body(i)
        return carry

    lax.fori_loop(0, count, step, 0)


def nearest(i, size):
    k = lax.div(i, 2) + 1
    return k + lax.rem(i, 2) * (size - 2 * k)


class Stage:
    def __init__(self, send_sems, recv_sems, base, count, to, landing):
        self.send_sems, self.recv_sems, self.base, self.count = send_sems, recv_sems, base, count
        self.to, self.landing = to, landing

    def copy(self, i, dst=None):
        src, there, device = self.to(i)
        return pltpu.make_async_remote_copy(
            src_ref=src,
            dst_ref=there if dst is None else dst,
            send_sem=self.send_sems.at[self.base + i],
            recv_sem=self.recv_sems.at[self.base + i],
            device_id=device,
            device_id_type=MESH,
        )

    def start(self, i):
        self.copy(i).start()

    def arrive(self, i):
        self.copy(i, self.landing(i)).wait_recv()

    def start_all(self):
        each(self.count, self.start)

    def arrive_all(self):
        each(self.count, self.arrive)

    def drain(self):
        each(self.count, lambda i: self.copy(i).wait_send())


def make_kernel(ys, zs, xs, far, hid):
    nodes = ys * zs * CORES
    chips = ys * zs
    blks = xs
    half = 16
    cf = 2 * half
    ch = hid // xs
    fin = cf * xs
    groups = zs * CORES
    lane_groups = hid // LANES
    tiles = 2 * (cf // 8) * lane_groups
    tiles_half = tiles // CORES
    per = tiles_half // zs
    bias_at = tiles_half * 8
    sem_plan = {}

    def plan(name, count):
        base = sum(c for _, c in sem_plan.values())
        sem_plan[name] = (base, count)

    for name, count in (
        ("a0", zs - 1), ("a1", ys - 1), ("b0", ys - 1), ("b1", zs - 1), ("c0", ys), ("c1", zs),
        ("halo", 2), ("xq", xs - 1), ("cq", xs - 1), ("ws", xs - 1), ("wn", xs - 1), ("bias", xs - 1),
        ("agg", xs - 1), ("scaled", xs - 1), ("hid", xs - 1), ("gl", xs - 1), ("bt", xs - 1),
        ("gc", 1), ("ga", zs - 1), ("gy", ys - 1), ("gz", groups - 1),
        ("core0", ys), ("core1", zs), ("p0", ys - 1), ("p1", zs - 1), ("r0", zs - 1), ("r1", ys - 1), ("out", 2),
    ):
        plan(name, count)
    n_sems = sum(c for _, c in sem_plan.values())

    scratch = dict(
        feat=((cf, blks * LANES), BF16), cot=((ch, blks * LANES), BF16), inv=((1, nodes), jnp.int32),
        srcs=((1, far), jnp.int32), bias_row=((1, ch), F32),
        hid_v=((ch, blks * LANES), BF16), gf_v=((cf, blks * LANES), BF16),
        gs_v=((cf, hid), F32), gn_v=((cf, hid), F32), gb_v=((1, ch), F32),
        XT=((blks, cf, LANES), BF16), xq=((xs, cf, LANES), BF16),
        cT=((blks, ch, LANES), BF16), cq=((xs, ch, LANES), BF16),
        wsF=((xs, cf, hid), BF16), wnF=((xs, cf, hid), BF16), biasF=((xs, 8, LANES), F32),
        wsT=((hid, fin), BF16), wnT=((hid, fin), BF16), pre0=((hid, LANES), F32),
        e0=((CORES, chips, half, LANES), BF16), e1=((CORES, chips, half, LANES), BF16),
        halo=((2, cf, LANES), BF16),
        A=((LANES, far * LANES), BF16), band=((blks, 3, LANES, LANES), BF16),
        Lm=((blks * cf + half, far * LANES), BF16),
        near=((blks, cf + half, LANES), F32), deg=((blks, 8, LANES), F32),
        agg=((blks, cf, LANES), BF16), aq=((xs, cf, LANES), BF16),
        ss=((xs, cf, LANES), BF16), sq=((blks, cf, LANES), BF16),
        stq=((blks, cf, LANES), F32), gl=((blks, hid, LANES), BF16), bt=((xs, 8, LANES), F32),
        hs=((xs, ch, LANES), BF16), hq=((blks, ch, LANES), BF16),
        gh=((CORES, bias_at + 8, LANES), F32), ghr=((bias_at + 8, LANES), F32),
        ga=((zs, per * 8 + lane_groups, LANES), F32), gar=((zs, per * 8 + lane_groups, LANES), F32),
        gb=((per * 8 + lane_groups, LANES), F32), gyr=((ys, per * 8 + lane_groups, LANES), F32),
        gt=((per * 8, LANES), F32), gzr=((groups, per * 8, LANES), F32),
        BK=((far, cf, LANES), F32),
        cs0=((chips, half, LANES), BF16), cs1=((chips, half, LANES), BF16),
        cr0=((chips, half, LANES), BF16), cr1=((chips, half, LANES), BF16),
        ps0=((chips, half, LANES), BF16), ps1=((chips, half, LANES), BF16),
        pr0=((ys, zs, half, LANES), BF16), pr1=((zs, ys, half, LANES), BF16),
        q0=((zs, half, LANES), F32), q1=((ys, half, LANES), F32),
        f0=((zs, half, LANES), F32), f1=((ys, half, LANES), F32),
        ho=((2, cf, LANES), F32), hr=((2, cf, LANES), F32),
        inner=((blks, cf, LANES), F32),
    )
    names = list(scratch)

    def kernel(
        row_hbm, src_hbm, eb_hbm, bias_hbm, srcs_hbm, feat_hbm, cot_hbm, ws_hbm, wn_hbm, band_hbm, far_hbm,
        hid_hbm, gf_hbm, gs_hbm, gn_hbm, gb_hbm, *rest,
    ):
        s = dict(zip(names, rest))
        send_sems, recv_sems, local_sems, inv_s, row_s, src_s, eb_s = rest[len(names):]
        hid_o, gf_o, gs_o, gn_o, gb_o = (s[name] for name in ("hid_v", "gf_v", "gs_v", "gn_v", "gb_v"))
        n = lax.axis_index("nodes")
        x = lax.axis_index("feat")
        c = lax.rem(n, CORES)
        z = lax.rem(lax.div(n, CORES), zs)
        y = lax.div(n, CORES * zs)
        o = 1 - c
        g_me = z * CORES + c

        def node(yy, zz, cc):
            return (yy * zs + zz) * CORES + cc

        def stage(name, to, landing):
            base, count = sem_plan[name]
            return Stage(send_sems, recv_sems, base, count, to, landing)

        def offset(i, size, far_first):
            return nearest(size - 2 - i if far_first else i, size)

        def along_z(name, src, there, here, far_first=False):
            def to(i):
                peer = lax.rem(z + offset(i, zs, far_first), zs)
                return src(peer), there(z), (node(y, peer, c), x)

            return stage(name, to, lambda i: here(lax.rem(z - offset(i, zs, far_first) + zs, zs)))

        def along_y(name, src, there, here, far_first=False):
            def to(i):
                peer = lax.rem(y + offset(i, ys, far_first), ys)
                return src(peer), there(y), (node(peer, z, c), x)

            return stage(name, to, lambda i: here(lax.rem(y - offset(i, ys, far_first) + ys, ys)))

        def across(i, size):
            return 1 + lax.rem(i + size // 2 - 1, size - 1)

        def along_x(name, src, land):
            def to(i):
                peer = lax.rem(x + across(i, xs), xs)
                return src(peer), land(x), (n, peer)

            return stage(name, to, lambda i: land(lax.rem(x - across(i, xs) + xs, xs)))

        def along_group(name, src, land):
            def to(i):
                peer = lax.rem(g_me + across(i, groups), groups)
                return src(peer), land(g_me), (node(y, lax.div(peer, CORES), lax.rem(peer, CORES)), x)

            return stage(name, to, lambda i: land(lax.rem(g_me - across(i, groups) + groups, groups)))

        left, right = lax.rem(n + nodes - 1, nodes), lax.rem(n + 1, nodes)

        def to_sides(name, first, last, land):
            def to(i):
                return (first, last)[i], land((1, 0)[i]), ((left, right)[i], x)

            class Sides(Stage):
                def start_all(self):
                    self.start(0)
                    self.start(1)

                def arrive_all(self):
                    self.arrive(0)
                    self.arrive(1)

                def drain(self):
                    for i in range(2):
                        self.copy(i).wait_send()

            base, count = sem_plan[name]
            return Sides(send_sems, recv_sems, base, count, to, lambda i: land((1, 0)[i]))

        def to_core(name, src, there, here):
            return stage(name, lambda i: (src(i), there(i), (node(y, z, o), x)), here)

        barrier = pltpu.get_barrier_semaphore()

        def greet(device):
            pl.semaphore_signal(barrier, inc=1, device_id=device, device_id_type=MESH)

        def greet_group(i):
            peer = lax.rem(g_me + across(i, groups), groups)
            greet((node(y, lax.div(peer, CORES), lax.rem(peer, CORES)), x))

        def fetch(src, dst, sem):
            one = pltpu.make_async_copy(src, dst, local_sems.at[sem])
            one.start()
            return one

        each(ys - 1, lambda i: greet((node(lax.rem(y + offset(i, ys, True), ys), z, c), x)))
        feat_copy = fetch(feat_hbm, s["feat"], 0)
        eb_copy = fetch(eb_hbm, eb_s, 7)
        each(groups - 1, greet_group)
        each(xs - 1, lambda i: greet((n, lax.rem(x + i + 1, xs))))
        greet((left, x))
        greet((right, x))
        ws_copy = fetch(ws_hbm, s["wsF"].at[x], 2)
        wn_copy = fetch(wn_hbm, s["wnF"].at[x], 3)
        cot_copy = fetch(cot_hbm, s["cot"], 1)
        bias_copy = fetch(bias_hbm, s["bias_row"], 8)
        srcs_copy = fetch(srcs_hbm, s["srcs"], 9)
        band_copy = fetch(band_hbm, s["band"], 4)
        row_copy = fetch(row_hbm, row_s, 10)
        src_copy = fetch(src_hbm, src_s, 11)

        feat_copy.wait()
        for b in range(blks):
            s["XT"][b] = s["feat"][:, b * LANES : (b + 1) * LANES]
        eb_copy.wait()
        eb = eb_s[0]
        mine = s["XT"][eb]
        s["e0"][c, y * zs + z] = mine[:half]
        s["e1"][c, z * ys + y] = mine[half:]

        pl.semaphore_wait(barrier, ys - 1 + groups - 1 + xs - 1 + 2)

        e0, e1 = s["e0"], s["e1"]
        a0 = along_z("a0", lambda p: e0.at[c, y * zs + z], *[lambda q: e0.at[c, y * zs + q]] * 2, far_first=True)
        a1 = along_y("a1", lambda p: e1.at[c, z * ys + y], *[lambda q: e1.at[c, z * ys + q]] * 2, far_first=True)
        a0.start_all()
        a1.start_all()
        halo = to_sides("halo", s["XT"].at[0], s["XT"].at[blks - 1], lambda i: s["halo"].at[i])
        halo.start_all()
        xq = along_x("xq", lambda p: s["XT"].at[p], lambda q: s["xq"].at[q])
        ws = along_x("ws", lambda p: s["wsF"].at[x], lambda q: s["wsF"].at[q])
        wn = along_x("wn", lambda p: s["wnF"].at[x], lambda q: s["wnF"].at[q])
        bias = along_x("bias", lambda p: s["biasF"].at[x], lambda q: s["biasF"].at[q])
        cq = along_x("cq", lambda p: s["cT"].at[p], lambda q: s["cq"].at[q])
        early = (xq, ws, wn, bias, cq)
        xq.start_all()
        ws_copy.wait()
        ws.start_all()
        wn_copy.wait()
        wn.start_all()
        cot_copy.wait()
        for b in range(blks):
            s["cT"][b] = s["cot"][:, b * LANES : (b + 1) * LANES]
        cq.start_all()
        s["biasF"][x] = jnp.zeros((8, LANES), F32)
        bias_copy.wait()
        s["biasF"][x, 0:1, 0:ch] = s["bias_row"][...]
        bias.start_all()
        s["xq"][x] = s["XT"][x]
        s["cq"][x] = s["cT"][x]

        def start_far(f):
            cols = pl.ds(pl.multiple_of(f * LANES, LANES), LANES)
            pltpu.make_async_copy(far_hbm.at[f], s["A"].at[:, cols], local_sems.at[5]).start()

        each(far, start_far)

        srcs_copy.wait()
        diagonal = lax.broadcasted_iota(jnp.int32, (far, far), 0) == lax.broadcasted_iota(jnp.int32, (far, far), 1)
        src_col = jnp.max(jnp.where(diagonal, s["srcs"][...], 0), axis=1, keepdims=True)
        owners = lax.broadcasted_iota(jnp.int32, (far, nodes), 1)
        index = lax.broadcasted_iota(jnp.int32, (far, nodes), 0)
        s["inv"][...] = jnp.max(jnp.where(src_col == owners, index, -1), axis=0, keepdims=True)
        inv_copy = pltpu.make_async_copy(s["inv"], inv_s, local_sems.at[6])
        inv_copy.start()

        def row0(q):
            return e0.at[c, pl.ds(q * zs, zs)]

        def row1(q):
            return e1.at[c, pl.ds(q * ys, ys)]

        b0 = along_y("b0", lambda p: row0(y), row0, row0, far_first=True)
        b1 = along_z("b1", lambda p: row1(z), row1, row1, far_first=True)

        def near_y(i):
            i = jnp.int32(i)
            return lax.rem(y - offset(jnp.maximum(i - 1, 0), ys, True) * jnp.minimum(i, 1) + ys, ys)

        def near_z(i):
            i = jnp.int32(i)
            return lax.rem(z - offset(jnp.maximum(i - 1, 0), zs, True) * jnp.minimum(i, 1) + zs, zs)

        c0 = to_core(
            "c0", lambda i: row0(near_y(i)), lambda i: row0(near_y(i)), lambda i: e0.at[o, pl.ds(near_y(i) * zs, zs)]
        )
        c1 = to_core(
            "c1", lambda i: row1(near_z(i)), lambda i: row1(near_z(i)), lambda i: e1.at[o, pl.ds(near_z(i) * ys, ys)]
        )
        a0.arrive_all()
        b0.start_all()
        c0.start(0)
        a1.arrive_all()
        b1.start_all()
        c1.start(0)

        band_copy.wait()
        halo.arrive_all()
        ones = jnp.ones((half, LANES), BF16)
        for b in range(blks):
            total = None
            for k in range(3):
                w = b + k - 1
                block = s["halo"][0] if w < 0 else s["halo"][1] if w >= blks else s["XT"][w]
                term = dot(jnp.concatenate([block, ones], 0), s["band"][b, k], 1, 1)
                total = term if total is None else total + term
            s["near"][b] = total
        for one in early:
            one.arrive_all()
        eye_w = eye(hid, BF16)
        w_self = s["wsF"][...].reshape(fin, hid)
        w_neigh = s["wnF"][...].reshape(fin, hid)
        s["wsT"][...] = dot(eye_w, w_self, 1, 1).astype(BF16)
        s["wnT"][...] = dot(eye_w, w_neigh, 1, 1).astype(BF16)
        x_full = s["xq"][...].reshape(fin, LANES)
        own_part = dot(s["wsT"][...], x_full, 1, 0)
        eye_h = eye(ch, F32)
        for q in range(xs):
            bias_col = jnp.sum(s["biasF"][q, 0:1, 0:ch] * eye_h, axis=1, keepdims=True)
            s["pre0"][q * ch : (q + 1) * ch] = own_part[q * ch : (q + 1) * ch] + bias_col
        far_all = pltpu.make_async_copy(s["A"], s["A"], local_sems.at[5])
        far_all.wait()
        inv_copy.wait()
        row_copy.wait()
        src_copy.wait()

        for one in (a0, a1, halo, *early):
            one.drain()
        def pass_on0(i):
            b0.arrive(i)
            c0.start(i + 1)

        def pass_on1(i):
            b1.arrive(i)
            c1.start(i + 1)

        each(ys - 1, pass_on0)
        each(zs - 1, pass_on1)
        c0.arrive_all()
        c1.arrive_all()

        iota = lax.broadcasted_iota(jnp.int32, (half, LANES), 0)
        zero = jnp.zeros((half, LANES), BF16)
        step = min(8, far)

        def place(f4):
            for k in range(step):
                f = f4 * step + k
                cols = pl.ds(pl.multiple_of(f * LANES, LANES), LANES)
                src = src_s[f]
                chip = lax.div(src, CORES)
                core = src - chip * CORES
                sy = lax.div(chip, zs)
                sz = chip - sy * zs
                lo = e0[core, chip]
                hi = e1[core, sz * ys + sy]
                row = row_s[f]
                for b in range(blks):
                    here = row == b
                    s["Lm"][b * cf : b * cf + half, cols] = lax.select(here, lo, zero)
                    s["Lm"][b * cf + half : (b + 1) * cf, cols] = lax.select(here, hi, zero)
                s["Lm"][blks * cf :, cols] = jnp.where(iota == row, 1.0, 0.0).astype(BF16)

        each(far // step, place)
        far_sum = dot(s["Lm"][...], s["A"][...], 1, 1)
        for b in range(blks):
            deg = s["near"][b, cf : cf + 8] + far_sum[blks * cf + b : blks * cf + b + 1]
            s["deg"][b] = deg
            summed = s["near"][b, :cf] + far_sum[b * cf : (b + 1) * cf]
            s["agg"][b] = (summed / deg[:1]).astype(BF16)
        agg = along_x("agg", lambda p: s["agg"].at[p], lambda q: s["aq"].at[q])
        agg.start_all()
        s["aq"][x] = s["agg"][x]
        deg_row = s["deg"][x][:1]
        for one in (b0, b1, c0, c1):
            one.drain()
        agg.arrive_all()

        agg_full = s["aq"][...].reshape(fin, LANES)
        pre = s["pre0"][...] + dot(s["wnT"][...], agg_full, 1, 0)
        sigma = jax.nn.sigmoid(pre)
        cot = s["cq"][...].reshape(hid, LANES).astype(F32)
        grad_pre = cot * sigma * (1.0 + pre * (1.0 - sigma))
        grad_low = grad_pre.astype(BF16)
        neigh = dot(s["wnF"][...].reshape(fin, hid), grad_low, 1, 0)
        s["ss"][...] = (neigh / deg_row).astype(BF16).reshape(xs, cf, LANES)
        scaled = along_x("scaled", lambda p: s["ss"].at[p], lambda q: s["sq"].at[q])
        scaled.start_all()
        s["sq"][x] = s["ss"][x]

        s["gl"][x] = grad_low
        gl = along_x("gl", lambda p: s["gl"].at[x], lambda q: s["gl"].at[q])
        gl.start_all()
        bias_row = dot(jnp.ones((8, LANES), F32), grad_pre, 1, 1, lax.Precision.HIGHEST)
        rows8 = lax.broadcasted_iota(jnp.int32, (8, LANES), 0)
        bias_tile = jnp.zeros((8, LANES), F32)
        for l in range(lane_groups):
            bias_tile = jnp.where(rows8 == l, bias_row[:, l * LANES : (l + 1) * LANES], bias_tile)
        s["bt"][x] = bias_tile
        bt = along_x("bt", lambda p: s["bt"].at[x], lambda q: s["bt"].at[q])
        bt.start_all()
        s["hs"][...] = (pre * sigma).astype(BF16).reshape(xs, ch, LANES)
        s["hq"][x] = s["hs"][x]

        for one in (agg,):
            one.drain()
        scaled.arrive_all()

        wide = min(16, far)

        def back(f16):
            for k in range(wide):
                f = f16 * wide + k
                cols = pl.ds(pl.multiple_of(f * LANES, LANES), LANES)
                s["BK"][f] = dot(s["sq"][row_s[f]], s["A"][:, cols], 1, 0)

        each(far // wide, back)

        gl.arrive_all()
        bt.arrive_all()
        grads = None
        for b in range(blks):
            both = jnp.concatenate([s["XT"][b], s["agg"][b]], 0)
            term = dot(both, s["gl"][b], 1, 1)
            grads = term if grads is None else grads + term
        t = 0
        for w in range(2):
            for r in range(cf // 8):
                for l in range(lane_groups):
                    at = w * cf + r * 8
                    row = t % tiles_half * 8
                    s["gh"][t // tiles_half, row : row + 8] = grads[at : at + 8, l * LANES : (l + 1) * LANES]
                    t += 1
        bias_sum = s["bt"][0]
        for q in range(1, xs):
            bias_sum = bias_sum + s["bt"][q]
        for k in range(CORES):
            s["gh"][k, bias_at:] = bias_sum
        gc = to_core("gc", lambda i: s["gh"].at[o], lambda i: s["ghr"], lambda i: s["ghr"])
        gc.start(0)

        def slot(owner):
            f = inv_s[0, owner]
            return jnp.minimum(jnp.maximum(f, 0), far - 1), (f >= 0).astype(F32)

        def share0(i):
            def one(k):
                at = i * zs + k
                f, there = slot(at * CORES + o)
                s["cs0"][at] = (s["BK"][f, :half] * there).astype(BF16)

            for k in range(zs):
                one(k)
            core0.start(i)

        def share1(i):
            for k in range(ys):
                f, there = slot((k * zs + i) * CORES + o)
                s["cs1"][i * ys + k] = (s["BK"][f, half:] * there).astype(BF16)
            core1.start(i)

        def of0(ref):
            return lambda i: ref.at[pl.ds(i * zs, zs)]

        def of1(ref):
            return lambda i: ref.at[pl.ds(i * ys, ys)]

        core0 = to_core("core0", of0(s["cs0"]), of0(s["cr0"]), of0(s["cr0"]))
        core1 = to_core("core1", of1(s["cs1"]), of1(s["cr1"]), of1(s["cr1"]))
        each(zs, share1)
        each(ys, share0)

        spread = [None] * (blks + 2)
        for b in range(blks):
            for k in range(3):
                term = dot(s["sq"][b], s["band"][b, k], 1, 0)
                spread[b + k] = term if spread[b + k] is None else spread[b + k] + term
        s["ho"][0] = spread[0]
        s["ho"][1] = spread[blks + 1]
        for b in range(blks):
            s["inner"][b] = spread[b + 1]
        outward = to_sides("out", s["ho"].at[0], s["ho"].at[1], lambda i: s["hr"].at[i])
        gc.arrive(0)
        for k in range(zs):
            rows = slice(k * per * 8, (k + 1) * per * 8)
            s["ga"][k, : per * 8] = s["gh"][c, rows] + s["ghr"][rows]
            bias_rows = slice(bias_at, bias_at + lane_groups)
            s["ga"][k, per * 8 :] = s["gh"][c, bias_rows] + s["ghr"][bias_rows]
        ga = along_z("ga", lambda p: s["ga"].at[p], *[lambda q: s["gar"].at[q]] * 2, far_first=True)
        ga.start_all()
        s["gar"][z] = s["ga"][z]
        outward.start_all()
        own_self = s["wsF"][x]
        for b in range(blks):
            s["stq"][b] = dot(own_self, s["gl"][b], 1, 0)

        p0 = along_y("p0", lambda p: s["ps0"].at[pl.ds(p * zs, zs)], *[lambda q: s["pr0"].at[q]] * 2, far_first=True)
        p1 = along_z("p1", lambda p: s["ps1"].at[pl.ds(p * ys, ys)], *[lambda q: s["pr1"].at[q]] * 2, far_first=True)

        def add0(i):
            core0.arrive(i)
            for k in range(zs):
                at = i * zs + k
                f, there = slot(at * CORES + c)
                s["ps0"][at] = (s["BK"][f, :half] * there + s["cr0"][at].astype(F32)).astype(BF16)

        def add1(i):
            core1.arrive(i)
            for k in range(ys):
                at = i * ys + k
                f, there = slot((k * zs + i) * CORES + c)
                s["ps1"][at] = (s["BK"][f, half:] * there + s["cr1"][at].astype(F32)).astype(BF16)

        each(zs, add1)
        p1.start_all()
        each(ys, add0)
        p0.start_all()
        s["pr0"][y] = s["ps0"][pl.ds(y * zs, zs)]
        s["pr1"][z] = s["ps1"][pl.ds(z * ys, ys)]

        ga.arrive_all()
        total = s["gar"][0]
        for g in range(1, zs):
            total = total + s["gar"][g]
        s["gb"][...] = total
        gy = along_y("gy", lambda p: s["gb"], *[lambda q: s["gyr"].at[q]] * 2, far_first=True)
        gy.start_all()
        s["gyr"][y] = total
        def add_up(ref, count):
            total = ref[0].astype(F32)
            for q in range(1, count):
                total = total + ref[q].astype(F32)
            return total

        for one in (scaled, gl, bt, gc, core0, core1, outward, ga):
            one.drain()
        gy.arrive_all()
        total = s["gyr"][0]
        for q in range(1, ys):
            total = total + s["gyr"][q]
        s["gt"][...] = total[: per * 8]
        gb_row = jnp.zeros((1, ch), F32)
        for q in range(xs):
            at = q * ch
            row = per * 8 + at // LANES
            part = total[row : row + 1, at % LANES : at % LANES + ch]
            gb_row = jnp.where(x == q, part, gb_row)
        gb_o[...] = gb_row
        gz = along_group("gz", lambda p: s["gt"], lambda q: s["gzr"].at[q])
        gz.start_all()
        s["gzr"][g_me] = total[: per * 8]

        p1.arrive_all()
        s["q1"][...] = add_up(s["pr1"], zs)
        r1 = along_y("r1", lambda p: s["q1"].at[p], *[lambda q: s["f1"].at[q]] * 2, far_first=True)
        r1.start_all()
        p0.arrive_all()
        s["q0"][...] = add_up(s["pr0"], ys)
        r0 = along_z("r0", lambda p: s["q0"].at[p], *[lambda q: s["f0"].at[q]] * 2, far_first=True)
        r0.start_all()
        s["f0"][z] = s["q0"][z]
        s["f1"][y] = s["q1"][y]

        hidden = along_x("hid", lambda p: s["hs"].at[p], lambda q: s["hq"].at[q])
        hidden.start_all()
        for one in (p0, p1, gy):
            one.drain()
        outward.arrive_all()
        gz.arrive_all()
        t = 0
        for out in (gs_o, gn_o):
            for r in range(cf // 8):
                for l in range(lane_groups):
                    out[r * 8 : (r + 1) * 8, l * LANES : (l + 1) * LANES] = s["gzr"][
                        t % tiles_half // per * CORES + t // tiles_half, t % per * 8 : t % per * 8 + 8
                    ]
                    t += 1
        gs_out = fetch(gs_o, gs_hbm, 13)
        gn_out = fetch(gn_o, gn_hbm, 14)
        gb_out = fetch(gb_o, gb_hbm, 15)
        hidden.arrive_all()
        for b in range(blks):
            hid_o[:, b * LANES : (b + 1) * LANES] = s["hq"][b]
        hid_out = fetch(hid_o, hid_hbm, 12)
        r1.arrive_all()
        r0.arrive_all()
        far_total = jnp.concatenate([add_up(s["f0"], zs), add_up(s["f1"], ys)], 0)
        for b in range(blks):
            value = s["inner"][b]
            if b == 0:
                value = value + s["hr"][0]
            if b == blks - 1:
                value = value + s["hr"][1]
            value = s["stq"][b] + value
            value = value + lax.select(eb == b, far_total, jnp.zeros_like(far_total))
            gf_o[:, b * LANES : (b + 1) * LANES] = value.astype(BF16)
        gf_out = fetch(gf_o, gf_hbm, 16)

        for one in (gz, r0, r1, hidden):
            one.drain()
        for one in (hid_out, gs_out, gn_out, gb_out, gf_out):
            one.wait()

    outs = (
        jax.ShapeDtypeStruct((ch, blks * LANES), BF16),
        jax.ShapeDtypeStruct((cf, blks * LANES), BF16),
        jax.ShapeDtypeStruct((cf, hid), F32),
        jax.ShapeDtypeStruct((cf, hid), F32),
        jax.ShapeDtypeStruct((1, ch), F32),
    )
    scratch_shapes = [pltpu.VMEM(shape, dtype) for shape, dtype in scratch.values()] + [
        pltpu.SemaphoreType.DMA((n_sems,)),
        pltpu.SemaphoreType.DMA((n_sems,)),
        pltpu.SemaphoreType.DMA((17,)),
        pltpu.SMEM((1, nodes), jnp.int32),
        pltpu.SMEM((far,), jnp.int32),
        pltpu.SMEM((far,), jnp.int32),
        pltpu.SMEM((1,), jnp.int32),
    ]
    vmem = pl.BlockSpec(memory_space=pltpu.VMEM)
    hbm = pl.BlockSpec(memory_space=pl.ANY)
    call = pl.pallas_call(
        kernel,
        out_shape=outs,
        in_specs=[hbm] * 11,
        out_specs=[hbm] * 5,
        scratch_shapes=scratch_shapes,
        compiler_params=pltpu.CompilerParams(
            collective_id=0, has_side_effects=True, vmem_limit_bytes=VMEM_LIMIT
        ),
        name="layer",
    )

    def pass_through(*refs):
        for i in range(5):
            refs[i + 5][...] = refs[i][...]

    finish = pl.pallas_call(
        pass_through,
        out_shape=outs,
        in_specs=[vmem] * 5,
        out_specs=[vmem] * 5,
        compiler_params=pltpu.CompilerParams(vmem_limit_bytes=VMEM_LIMIT),
        name="pass_through",
    )
    return call, finish


def solution(mesh):
    nodes, xs = mesh.shape["nodes"], mesh.shape["feat"]
    ys, zs = sides(nodes)

    def on_device(
        features, band_counts, far_counts, far_row, far_src, export_block, w_self, w_neigh, bias, cotangent
    ):
        far = far_counts.shape[0]
        hid = w_self.shape[1]
        call, finish = make_kernel(ys, zs, xs, far, hid)
        parts = call(
            far_row, far_src, export_block, bias.reshape(1, -1), far_src.reshape(1, -1), features.T, cotangent.T,
            w_self, w_neigh, band_counts, far_counts,
        )
        hidden, grad_features, grad_self, grad_neigh, grad_bias = finish(*parts)
        return hidden.T, grad_features.T, grad_self, grad_neigh, grad_bias.reshape(bias.shape)

    return jax.shard_map(
        on_device,
        mesh=mesh,
        in_specs=(
            P("nodes", "feat"),
            P("nodes", None, None, None),
            P("nodes", None, None),
            P("nodes"),
            P("nodes"),
            P("nodes"),
            P("feat", None),
            P("feat", None),
            P("feat"),
            P("nodes", "feat"),
        ),
        out_specs=(
            P("nodes", "feat"),
            P("nodes", "feat"),
            P("feat", None),
            P("feat", None),
            P("feat"),
        ),
        check_vma=False,
    )
```
